256 devices in a mesh: pair: 4 (over x), row: 64 (over z, y, core).
Axes of the slice: x: 4, y: 4, z: 8, core: 2. Of those that a mesh axis runs over, the one named last changes fastest.
Arguments:
- matrix: float32 [16384, 4096], P('row', 'pair'), may hold values from -18 to 18, as said below
- plan: int32 [2, 8], replicated, may hold values from 0 to 7, each once within a row
Outputs:
- rotated: float32 [16384, 4096], P('row', 'pair')
The draws below stay inside these ranges and needn't reach their ends.
Inputs may be any that keep to these rules, and one draw needn't show every extreme that they name: `matrix`: an entry's magnitude is at most 18. `plan`: each row names every block number once.
All inputs are finite; a program needn't handle non-finite values.
Results may differ from the reference program's by a relative error of at most 0.0004.
Values sent between devices are 32-bit elements; how exact they have to be, the bound alone decides.
A program may use at most 128 MiB of HBM per device.

```python
import math
import jax
import jax.numpy as jnp
from jax import lax

B = 512
ROUNDS = 2
BLOCKS = 8
NCOLS = 4096
ROWS = 16384
N_PAIR = 4


def draw_matrix(key, part):
    key = jax.random.fold_in(key, 11)
    key_entries, key_cols = jax.random.split(key, 2)
    col_scale = jnp.exp(jax.random.uniform(key_cols, (1, NCOLS), jnp.float32, math.log(0.3), math.log(3.0)))
    entries = jax.random.truncated_normal(key_entries, -6.0, 6.0, (ROWS, NCOLS), jnp.float32)
    return entries * col_scale


def setup_inputs(seed: int = 0) -> dict:
    key_of = jax.random.split(jax.random.key(seed), 3)
    return {
        "matrix": draw_matrix(jax.random.fold_in(key_of[2], 71), 0),
        "plan": jax.vmap(lambda own: jax.random.permutation(own, BLOCKS))(jax.random.split(key_of[1], ROUNDS)).reshape((ROUNDS, BLOCKS)).astype(jnp.int32),
    }


def rotate_pair(pair_rows):
    width = pair_rows.shape[1]
    gram_sum = jnp.dot(pair_rows.T.astype(jnp.float32), pair_rows.astype(jnp.float32), precision=lax.Precision.HIGHEST, preferred_element_type=jnp.float32)
    ramp_values = jnp.arange(width).astype(jnp.float32) / width
    skew_part = gram_sum * (ramp_values[None, :] - ramp_values[:, None]) / math.sqrt(ROWS)
    square = jnp.dot(skew_part.astype(jnp.float32), skew_part.astype(jnp.float32), precision=lax.Precision.HIGHEST, preferred_element_type=jnp.float32)
    identity_mat = jnp.eye(width, dtype=jnp.float32)
    core_matrix = identity_mat - 0.25 * square
    numer = identity_mat + skew_part + 0.25 * square
    lower_factor = jnp.linalg.cholesky(core_matrix)
    half_solved = lax.linalg.triangular_solve(lower_factor, numer, left_side=True, lower=True)
    rotation = lax.linalg.triangular_solve(lower_factor, half_solved, left_side=True, lower=True, transpose_a=True)
    return jnp.dot(pair_rows.astype(jnp.float32), rotation.astype(jnp.float32), precision=lax.Precision.HIGHEST, preferred_element_type=jnp.float32)

def reference(matrix, plan):
    blocks = matrix.reshape(ROWS, BLOCKS, B)
    holders = jnp.arange(BLOCKS).astype(jnp.int32)
    for round_index in range(ROUNDS):
        pairs = jnp.transpose(blocks.reshape(ROWS, N_PAIR, 2 * B), (1, 0, 2))
        turned = lax.map(rotate_pair, pairs)
        turned = jnp.transpose(turned, (1, 0, 2)).reshape(ROWS, BLOCKS, B)
        places = jnp.zeros((BLOCKS,), jnp.int32).at[holders].set(jnp.arange(BLOCKS).astype(jnp.int32))
        targets = plan[round_index]
        blocks = jnp.take(turned, places[targets], axis=1)
        holders = targets
    return blocks.reshape(ROWS, NCOLS)
```

```python
import functools

import jax
import jax.numpy as jnp
from jax import lax
from jax.experimental import pallas as pl
from jax.experimental.pallas import tpu as pltpu
from jax.sharding import PartitionSpec as P

ROUNDS = 2
F32 = jnp.float32
BF = jnp.bfloat16
MESH = pl.DeviceIdType.MESH
BLK = [(i, j) for i in range(8) for j in range(i, 8)]
NZ, NY = 8, 4
HALF, QUART, PIECE = 2304, 576, 72


def lb(x, c):
    return jnp.broadcast_to(x[:, c:c+1], (8,128))
def sb(x, s):
    return jnp.broadcast_to(x[s:s+1, :], (8,128))

def inv128(M, sub, lane, nb=16):
    M=list(M)
    for p in range(nb):
        R=[[lb(M[r],8*p+k) for k in range(8)] for r in [p]][0]
        E=list(R)
        inpan=(lane>=8*p)&(lane<8*p+8)
        for s in range(0,8,2):
            a=sb(E[s],s); b=sb(E[s+1],s); c=sb(E[s],s+1); d=sb(E[s+1],s+1)
            rd=1.0/(a*d-b*c)
            r0=sub==s; r1=sub==s+1
            ps,pq=E[s],E[s+1]
            new=list(E)
            for j in range(8):
                if j in (s,s+1): continue
                t0=sb(E[j],s); t1=sb(E[j],s+1)
                T0=(d*t0-b*t1)*rd
                T1=(a*t1-c*t0)*rd
                new[j]=jnp.where(r0,T0,jnp.where(r1,T1,E[j]-ps*T0-pq*T1))
            i00=d*rd; i01=-b*rd; i10=-c*rd; i11=a*rd
            new[s]=jnp.where(r0,i00,jnp.where(r1,i10,-(ps*i00+pq*i10)))
            new[s+1]=jnp.where(r0,i01,jnp.where(r1,i11,-(ps*i01+pq*i11)))
            E=new
        Mp=jnp.where(inpan,jnp.where(lane-8*p==sub,1.0,0.0),M[p])
        t=[E[k]*sb(Mp,k) for k in range(8)]
        N=((t[0]+t[1])+(t[2]+t[3]))+((t[4]+t[5])+(t[6]+t[7]))
        Nb=[sb(N,k) for k in range(8)]
        for r in range(nb):
            if r==p: continue
            base=jnp.where(inpan,0.0,M[r])
            t=[lb(M[r],8*p+k)*Nb[k] for k in range(8)]
            M[r]=base-(((t[0]+t[1])+(t[2]+t[3]))+((t[4]+t[5])+(t[6]+t[7])))
        M[p]=N
    return M

def split(x):
    hi=x.astype(BF); lo=(x-hi.astype(F32)).astype(BF)
    return hi,lo
def dot(a,b): return jnp.dot(a,b,preferred_element_type=F32)

def gram_kern(p_ref,g_ref,ph,plo,th,tl):
    for c in range(0,1024,256):
        x=p_ref[:,c:c+256]
        hi,lo=split(x)
        ph[:,c:c+256]=hi; plo[:,c:c+256]=lo
        xt=x.T
        hi,lo=split(xt)
        th[c:c+256,:]=hi; tl[c:c+256,:]=lo
    for bi in range(4):
        r=slice(256*bi,256*bi+256)
        for bj in range(bi,4):
            c=slice(256*bj,256*bj+256)
            g=dot(th[r,:],ph[:,c])+(dot(th[r,:],plo[:,c])+dot(tl[r,:],ph[:,c]))
            for u in range(2):
                for v in range(2):
                    ij=(2*bi+u,2*bj+v)
                    if ij in BLK:
                        n=BLK.index(ij)
                        g_ref[128*n:128*n+128,:]=g[128*u:128*u+128,128*v:128*v+128]

def gram(p):
    return pl.pallas_call(gram_kern,out_shape=jax.ShapeDtypeStruct((4608,128),F32),
      in_specs=[pl.BlockSpec(memory_space=pltpu.VMEM)],out_specs=pl.BlockSpec(memory_space=pltpu.VMEM),
      scratch_shapes=[pltpu.VMEM((256,1024),BF)]*2+[pltpu.VMEM((1024,256),BF)]*2,
      compiler_params=pltpu.CompilerParams(vmem_limit_bytes=60*2**20),name="gram")(p)

def solve_kern(parts,g_ref,p_ref,o_ref,c_ref,d_ref,dh_ref,dl_ref,ah_ref,al_ref):
    sub=lax.broadcasted_iota(jnp.int32,(8,128),0); lane=lax.broadcasted_iota(jnp.int32,(8,128),1)
    bi=lax.broadcasted_iota(jnp.int32,(128,128),0); bj=lax.broadcasted_iota(jnp.int32,(128,128),1)
    dif=(bj-bi).astype(F32)
    eye=jnp.where(bi==bj,1.0,0.0)
    for n,(i,j) in enumerate(BLK):
        k=g_ref[128*n:128*n+128,:]*((dif+128.0*(j-i))*(1.0/(1024*128*2)))
        if i==j:
            c_ref[128*i:128*i+128,128*i:128*i+128]=eye-k
        else:
            c_ref[128*i:128*i+128,128*j:128*j+128]=-k
            c_ref[128*j:128*j+128,128*i:128*i+128]=k.T
    c_ref[1024:1280,:]=p_ref[...]
    def step(k,_):
        k0=pl.multiple_of(k*128,128)
        kc=pl.ds(k0,128)
        if "inv" in parts:
            M=[c_ref[pl.ds(k0+8*r,8),kc] for r in range(16)]
            M=inv128(M,sub,lane)
            for r in range(16): d_ref[8*r:8*r+8,:]=M[r]
        c_ref[kc,kc]=jnp.zeros((128,128),F32)
        hi,lo=split(d_ref[...])
        dh_ref[...]=hi; dl_ref[...]=lo
        for c in range(0,1024,256):
            hi,lo=split(c_ref[kc,c:c+256])
            ah_ref[:,c:c+256]=hi; al_ref[:,c:c+256]=lo
        def rows(i,_):
            r=pl.ds(pl.multiple_of(i*128,128),128)
            xh,xl=split(c_ref[r,kc])
            y=dot(xh,dh_ref[...])+(dot(xh,dl_ref[...])+dot(xl,dh_ref[...]))
            yh,yl=split(y)
            for c in range(0,1024,256):
                cs=slice(c,c+256)
                c_ref[r,cs]=c_ref[r,cs]-(dot(yh,ah_ref[:,cs])+(dot(yh,al_ref[:,cs])+dot(yl,ah_ref[:,cs])))
            c_ref[r,kc]=y
            return 0
        if "upd" in parts:
            lax.fori_loop(k+1,10,rows,0)
        return 0
    lax.fori_loop(0,8,step,0)
    o_ref[...]=2.0*c_ref[1024:1280,:]-p_ref[...]

def solve(g,p,parts=("inv","upd")):
    import functools
    return pl.pallas_call(functools.partial(solve_kern,parts),out_shape=jax.ShapeDtypeStruct((256,1024),F32),
      in_specs=[pl.BlockSpec(memory_space=pltpu.VMEM)]*2,out_specs=pl.BlockSpec(memory_space=pltpu.VMEM),
      scratch_shapes=[pltpu.VMEM((1280,1024),F32),pltpu.VMEM((128,128),F32),pltpu.VMEM((128,128),BF),pltpu.VMEM((128,128),BF),pltpu.VMEM((128,1024),BF),pltpu.VMEM((128,1024),BF)],
      compiler_params=pltpu.CompilerParams(vmem_limit_bytes=60*2**20),name="solve")(g,p)

def comm_kern(g_ref,o_ref,r1,r2,r3,h,q,s1,v1,s2,v2,s3,v3,s4,v4,s5,v5,s6,v6):
    row=lax.axis_index("row")
    c=lax.rem(row,2); y=lax.rem(row//2,NY); z=row//(2*NY)
    def dev(zz,yy,cc): return {"row":(zz*NY+yy)*2+cc}
    other=dev(z,y,1-c)
    ys=[lax.rem(y+d,NY) for d in range(NY)]
    zs=[lax.rem(z+d,NZ) for d in range(NZ)]
    ydev=[dev(z,ys[d],c) for d in range(NY)]
    zdev=[dev(zs[d],y,c) for d in range(NZ)]
    bar=pltpu.get_barrier_semaphore()
    for t in [other]+ydev[1:]+zdev[1:]:
        pl.semaphore_signal(bar,inc=1,device_id=t,device_id_type=MESH)
    pl.semaphore_wait(bar,1+(NY-1)+(NZ-1))
    def rc(src,dst,ss,rs,t):
        return pltpu.make_async_remote_copy(src_ref=src,dst_ref=dst,send_sem=ss,recv_sem=rs,device_id=t,device_id_type=MESH)
    order=[1,3,2,0]
    c1=[]
    for d in order:
        yo=pl.multiple_of(ys[d]*QUART,8)
        cp=rc(g_ref.at[pl.ds(pl.multiple_of((1-c)*HALF+yo,8),QUART)],r1.at[pl.ds(yo,QUART)],s1.at[d],v1.at[d],other)
        cp.start(); c1.append(cp)
    c2=[]
    for n,d in enumerate(order):
        yo=pl.multiple_of(ys[d]*QUART,8)
        c1[n].wait_recv()
        h[pl.ds(yo,QUART),:]=g_ref[pl.ds(pl.multiple_of(c*HALF+yo,8),QUART),:]+r1[pl.ds(yo,QUART),:]
        if d:
            cp=rc(h.at[pl.ds(yo,QUART)],r2.at[d-1],s2.at[d-1],v2.at[d-1],ydev[d])
            cp.start(); c2.append(cp)
    for cp in c2: cp.wait_recv()
    c3=[]
    yo=pl.multiple_of(y*QUART,8)
    for d in [4,3,5,2,6,1,7,0]:
        zo=pl.multiple_of(zs[d]*PIECE,8)
        zr=pl.ds(zo,PIECE)
        q[zr,:]=(h[pl.ds(pl.multiple_of(yo+zo,8),PIECE),:]+r2[0,zr,:])+(r2[1,zr,:]+r2[2,zr,:])
        if d:
            cp=rc(q.at[zr],r3.at[d-1],s3.at[d-1],v3.at[d-1],zdev[d])
            cp.start(); c3.append(cp)
    zr=pl.ds(pl.multiple_of(z*PIECE,8),PIECE)
    for cp in c3: cp.wait_recv()
    t=q[zr,:]
    for d in range(NZ-1): t=t+r3[d]
    mine=pl.ds(pl.multiple_of(c*HALF+yo+z*PIECE,8),PIECE)
    o_ref[mine,:]=t
    c4=[]
    for d in [4,3,5,2,6,1,7]:
        cp=rc(o_ref.at[mine],o_ref.at[mine],s4.at[d-1],v4.at[d-1],zdev[d])
        cp.start(); c4.append(cp)
    for cp in c4: cp.wait_recv()
    quarter=pl.ds(pl.multiple_of(c*HALF+yo,8),QUART)
    c5=[];c6=[]
    for d in [1,3,2]:
        cp=rc(o_ref.at[quarter],o_ref.at[quarter],s5.at[d-1],v5.at[d-1],ydev[d])
        cp.start(); c5.append(cp)
    cp=rc(o_ref.at[quarter],o_ref.at[quarter],s6.at[0],v6.at[0],other)
    cp.start(); c6.append(cp)
    for n,d in enumerate([1,3,2]):
        c5[n].wait_recv()
        src=pl.ds(pl.multiple_of(c*HALF+lax.rem(y+NY-d,NY)*QUART,8),QUART)
        cp=rc(o_ref.at[src],o_ref.at[src],s6.at[d],v6.at[d],other)
        cp.start(); c6.append(cp)
    for cp in c6: cp.wait_recv()
    for cp in c1+c2+c3+c4+c5+c6: cp.wait_send()

def comm(g):
    D=pltpu.SemaphoreType.DMA
    return pl.pallas_call(comm_kern,out_shape=jax.ShapeDtypeStruct((4608,128),F32),
      in_specs=[pl.BlockSpec(memory_space=pltpu.VMEM)],out_specs=pl.BlockSpec(memory_space=pltpu.VMEM),
      scratch_shapes=[pltpu.VMEM((HALF,128),F32),pltpu.VMEM((3,QUART,128),F32),pltpu.VMEM((7,PIECE,128),F32),pltpu.VMEM((HALF,128),F32),pltpu.VMEM((QUART,128),F32)]
        +[D((4,)),D((4,)),D((3,)),D((3,)),D((7,)),D((7,)),D((7,)),D((7,)),D((3,)),D((3,)),D((4,)),D((4,))],
      compiler_params=pltpu.CompilerParams(vmem_limit_bytes=60*2**20,collective_id=0,has_side_effects=True),name="comm")(g)

def body(matrix, plan):
    rows_local, width = matrix.shape
    half_width = width // 2
    pair_index = lax.axis_index("pair")
    blocks_total = plan.shape[1]
    holders = jnp.arange(blocks_total)
    numbers = jnp.arange(blocks_total)
    pair_rows = matrix
    for round_index in range(ROUNDS):
        turned = solve(comm(gram(pair_rows)), pair_rows)
        gathered = lax.all_gather(turned, "pair", axis=1, tiled=True)
        gathered = gathered.reshape(rows_local, blocks_total, half_width)
        targets = plan[round_index]
        wanted = lax.dynamic_slice_in_dim(targets, 2 * pair_index, 2, 0)
        matches = holders[None, :] == wanted[:, None]
        places = jnp.sum(jnp.where(matches, numbers[None, :], 0), axis=1)
        pair_rows = jnp.take(gathered, places, axis=1).reshape(rows_local, width)
        holders = targets
    return pair_rows


def solution(mesh):
    placed = (P("row", "pair"), P())
    return jax.shard_map(
        body, mesh=mesh, in_specs=placed, out_specs=P("row", "pair"), check_vma=False
    )
```

```python
import functools
import itertools

import jax
import jax.numpy as jnp
from jax import lax
from jax.experimental import pallas as pl
from jax.experimental.pallas import tpu as pltpu
from jax.sharding import PartitionSpec as P

F32 = jnp.float32
BF = jnp.bfloat16
MESH = pl.DeviceIdType.MESH
OFF = [(i, j) for i in range(8) for j in range(i + 1, 8)]
NZ, NY = 8, 4
HALF, PA, PB = 2048, 1536, 512
YA, ZA, ZB, YB = PA // NY, PA // NY // NZ, PB // NZ, PB // NZ // NY
ZORDER = (4, 3, 5, 2, 6, 1, 7)


def lb(x, c):
    return jnp.broadcast_to(x[:, c:c+1], (8,128))
def sb(x, s):
    return jnp.broadcast_to(x[s:s+1, :], (8,128))

def inv128(M, sub, lane, nb=16):
    M=list(M)
    for p in range(nb):
        R=[[lb(M[r],8*p+k) for k in range(8)] for r in [p]][0]
        E=list(R)
        inpan=(lane>=8*p)&(lane<8*p+8)
        for s in range(0,8,2):
            a=sb(E[s],s); b=sb(E[s+1],s); c=sb(E[s],s+1); d=sb(E[s+1],s+1)
            rd=1.0/(a*d-b*c)
            r0=sub==s; r1=sub==s+1
            ps,pq=E[s],E[s+1]
            new=list(E)
            for j in range(8):
                if j in (s,s+1): continue
                t0=sb(E[j],s); t1=sb(E[j],s+1)
                T0=(d*t0-b*t1)*rd
                T1=(a*t1-c*t0)*rd
                new[j]=jnp.where(r0,T0,jnp.where(r1,T1,E[j]-ps*T0-pq*T1))
            i00=d*rd; i01=-b*rd; i10=-c*rd; i11=a*rd
            new[s]=jnp.where(r0,i00,jnp.where(r1,i10,-(ps*i00+pq*i10)))
            new[s+1]=jnp.where(r0,i01,jnp.where(r1,i11,-(ps*i01+pq*i11)))
            E=new
        Mp=jnp.where(inpan,jnp.where(lane-8*p==sub,1.0,0.0),M[p])
        t=[E[k]*sb(Mp,k) for k in range(8)]
        N=((t[0]+t[1])+(t[2]+t[3]))+((t[4]+t[5])+(t[6]+t[7]))
        Nb=[sb(N,k) for k in range(8)]
        for r in range(nb):
            if r==p: continue
            base=jnp.where(inpan,0.0,M[r])
            t=[lb(M[r],8*p+k)*Nb[k] for k in range(8)]
            M[r]=base-(((t[0]+t[1])+(t[2]+t[3]))+((t[4]+t[5])+(t[6]+t[7])))
        M[p]=N
    return M

def split(x):
    hi = x.astype(BF)
    return hi, (x - hi.astype(F32)).astype(BF)


def dot(a, b):
    return jnp.dot(a, b, preferred_element_type=F32)


def iotas(n, m):
    shape = (n, m)
    return lax.broadcasted_iota(jnp.int32, shape, 0), lax.broadcasted_iota(jnp.int32, shape, 1)


def vmem_call(kern, outs, n_smem, scratch, name, *args):
    vm = pl.BlockSpec(memory_space=pltpu.VMEM)
    sm = pl.BlockSpec(memory_space=pltpu.SMEM)
    return pl.pallas_call(
        kern,
        out_shape=outs,
        in_specs=[sm] * n_smem + [vm] * (len(args) - n_smem),
        out_specs=jax.tree.map(lambda _: vm, outs),
        scratch_shapes=scratch,
        compiler_params=pltpu.CompilerParams(vmem_limit_bytes=56 * 2**20),
        name=name,
    )(*args)


def load_pair(t_ref, parts, dst, row0):
    if len(parts) == 1:
        dst[row0:row0 + 256, :] = parts[0][...]
        return
    at = t_ref[4] * 512
    dst[row0:row0 + 256, pl.ds(pl.multiple_of(at, 512), 512)] = parts[0][...]
    dst[row0:row0 + 256, pl.ds(pl.multiple_of(512 - at, 512), 512)] = parts[1][...]


def gram_kern(n_parts, t_ref, *refs):
    parts = refs[:n_parts]
    g_ref, x_ref, ph, plo, th, tl = refs[n_parts:]
    load_pair(t_ref, parts, x_ref, 0)
    for c in range(0, 1024, 256):
        x = x_ref[:, c:c + 256]
        ph[:, c:c + 256], plo[:, c:c + 256] = split(x)
        th[c:c + 256, :], tl[c:c + 256, :] = split(x.T)
    bi, bj = iotas(128, 128)
    for i in range(4):
        r = slice(256 * i, 256 * i + 256)
        for j in range(i, 4):
            c = slice(256 * j, 256 * j + 256)
            g = dot(th[r, :], ph[:, c]) + (dot(th[r, :], plo[:, c]) + dot(tl[r, :], ph[:, c]))
            for u in range(2):
                for v in range(2):
                    if (2 * i + u, 2 * j + v) in OFF:
                        n = 128 * OFF.index((2 * i + u, 2 * j + v))
                        g_ref[n:n + 128, :] = g[128 * u:128 * u + 128, 128 * v:128 * v + 128]
            if i == j:
                n = 128 * (28 + i)
                g_ref[n:n + 128, :] = jnp.where(bj > bi, g[:128, :128], g[128:, 128:])


def gram(t, parts):
    return vmem_call(
        functools.partial(gram_kern, len(parts)),
        jax.ShapeDtypeStruct((4096, 128), F32),
        1,
        [pltpu.VMEM((256, 1024), F32)] + [pltpu.VMEM((256, 1024), BF)] * 2 + [pltpu.VMEM((1024, 256), BF)] * 2,
        "gram", t, *parts)


def solve_kern(n_parts, which, t_ref, g_ref, *refs):
    parts = refs[:n_parts]
    o0_ref, o1_ref, c_ref, d_ref, w_ref, wh_ref, wl_ref = refs[n_parts:]
    sub, lane = iotas(8, 128)
    bi, bj = iotas(128, 128)
    dif = (bj - bi).astype(F32)
    eye = jnp.where(bi == bj, 1.0, 0.0)
    scale = 1.0 / (1024 * 128 * 2)
    for n, (i, j) in enumerate(OFF):
        k = g_ref[128 * n:128 * n + 128, :] * ((dif + 128.0 * (j - i)) * scale)
        c_ref[128 * i:128 * i + 128, 128 * j:128 * j + 128] = -k
        c_ref[128 * j:128 * j + 128, 128 * i:128 * i + 128] = k.T
    for m in range(4):
        k = g_ref[128 * (28 + m):128 * (29 + m), :] * (dif * scale)
        up = jnp.where(bj > bi, k, 0.0)
        low = jnp.where(bj < bi, k, 0.0)
        a = 256 * m
        c_ref[a:a + 128, a:a + 128] = eye - (up - up.T)
        c_ref[a + 128:a + 256, a + 128:a + 256] = eye - (low - low.T)
    load_pair(t_ref, parts, c_ref, 1024)

    def step(k, _):
        k0 = pl.multiple_of(k * 128, 128)
        kc = pl.ds(k0, 128)
        m = inv128([c_ref[pl.ds(k0 + 8 * r, 8), kc] for r in range(16)], sub, lane)
        for r in range(16):
            d_ref[8 * r:8 * r + 8, :] = m[r]
        c_ref[kc, kc] = jnp.zeros((128, 128), F32)
        dh, dl = split(d_ref[...])
        w_ref[0:128, 0:128] = dh
        w_ref[128:256, 0:128] = dh
        w_ref[0:128, 128:256] = dl
        w_ref[128:256, 128:256] = dl
        for c in range(0, 1024, 256):
            hi, lo = split(c_ref[kc, c:c + 256])
            wh_ref[0:128, c:c + 256] = hi
            wh_ref[128:256, c:c + 256] = hi
            wl_ref[0:128, c:c + 256] = lo
            wl_ref[128:256, c:c + 256] = lo

        def rows(i, _):
            r = pl.ds(pl.multiple_of(i * 256, 256), 256)
            y = dot(jnp.concatenate(split(c_ref[r, kc]), axis=1), w_ref[...])
            y = y[:, :128] + y[:, 128:]
            y2 = jnp.concatenate(split(y), axis=1)
            for c in range(0, 1024, 256):
                cs = slice(c, c + 256)
                c_ref[r, cs] = c_ref[r, cs] - (dot(y2, wh_ref[:, cs]) + dot(y2, wl_ref[:, cs]))
            c_ref[r, kc] = y
            return 0

        lax.fori_loop((k + 1) // 2, 5, rows, 0)
        return 0

    lax.fori_loop(0, 8, step, 0)
    for n, o_ref in enumerate((o0_ref, o1_ref)):
        half = t_ref[which] if n == 0 else 1 - t_ref[which]
        cs = pl.ds(pl.multiple_of(half * 512, 512), 512)
        if n_parts == 1:
            old = parts[0][:, cs]
        else:
            old = jnp.where(half == t_ref[4], parts[0][...], parts[1][...])
        o_ref[...] = 2.0 * c_ref[1024:1280, cs] - old


def solve(t, g, parts, which):
    return vmem_call(
        functools.partial(solve_kern, len(parts), which),
        (jax.ShapeDtypeStruct((256, 512), F32),) * 2,
        1,
        [pltpu.VMEM((1280, 1024), F32), pltpu.VMEM((128, 128), F32), pltpu.VMEM((256, 256), BF)]
        + [pltpu.VMEM((256, 1024), BF)] * 2,
        "solve", t, g, *parts)


def comm_kern(g_ref, o_ref, r1, h, r2a, r2b, qa, qb, r3a, r3b, *sems):
    row = lax.axis_index("row")
    c = lax.rem(row, 2)
    y = lax.rem(row // 2, NY)
    z = row // (2 * NY)
    ys = [lax.rem(y + d, NY) for d in range(NY)]
    zs = [lax.rem(z + d, NZ) for d in range(NZ)]
    ydev = [{"row": (z * NY + ys[d]) * 2 + c} for d in range(NY)]
    zdev = [{"row": (zs[d] * NY + y) * 2 + c} for d in range(NZ)]
    other = {"row": (z * NY + y) * 2 + 1 - c}
    half = c * HALF

    def at(start, size):
        return pl.ds(pl.multiple_of(start, 8), size)

    barrier = pltpu.get_barrier_semaphore()
    for target in [other] + ydev[1:] + zdev[1:]:
        pl.semaphore_signal(barrier, inc=1, device_id=target, device_id_type=MESH)
    pl.semaphore_wait(barrier, NY + NZ - 1)

    sent = []

    def send(src, dst, pair, n, target):
        copy = pltpu.make_async_remote_copy(
            src_ref=src, dst_ref=dst, send_sem=sems[2 * pair].at[n], recv_sem=sems[2 * pair + 1].at[n],
            device_id=target, device_id_type=MESH)
        copy.start()
        sent.append(copy)
        return copy

    chunks = [at(ys[d] * YA, YA) for d in (1, 3, 2)] + [at(PA, PB), at(y * YA, YA)]
    core = [send(g_ref.at[at((1 - c) * HALF + s.start, s.size)], r1.at[s], 0, n, other) for n, s in enumerate(chunks)]

    def add(s):
        h[s, :] = g_ref[at(half + s.start, s.size), :] + r1[s, :]

    sums_ya, sums_zb = [], []
    for n, d in enumerate((1, 3, 2)):
        core[n].wait_recv()
        add(chunks[n])
        sums_ya.append(send(h.at[chunks[n]], r2a.at[d - 1], 1, d - 1, ydev[d]))
    core[3].wait_recv()
    for d in ZORDER:
        s = at(PA + zs[d] * ZB, ZB)
        add(s)
        sums_zb.append(send(h.at[s], r2b.at[d - 1], 2, d - 1, zdev[d]))
    add(at(PA + z * ZB, ZB))
    core[4].wait_recv()
    add(chunks[4])

    for copy in sums_zb:
        copy.wait_recv()
    total = h[at(PA + z * ZB, ZB), :]
    for d in range(NZ - 1):
        total = total + r2b[d]
    qb[...] = total
    sums_yb = [send(qb.at[at(ys[d] * YB, YB)], r3b.at[d - 1], 3, d - 1, ydev[d]) for d in (2, 1, 3)]

    for copy in sums_ya:
        copy.wait_recv()
    sums_za = []
    for d in ZORDER + (0,):
        s = at(zs[d] * ZA, ZA)
        qa[s, :] = (h[at(y * YA + zs[d] * ZA, ZA), :] + r2a[0, s, :]) + (r2a[1, s, :] + r2a[2, s, :])
        if d:
            sums_za.append(send(qa.at[s], r3a.at[d - 1], 4, d - 1, zdev[d]))

    for copy in sums_yb:
        copy.wait_recv()
    mine = at(half + PA + z * ZB + y * YB, YB)
    o_ref[mine, :] = (qb[at(y * YB, YB), :] + r3b[0]) + (r3b[1] + r3b[2])
    back_yb = [send(o_ref.at[mine], o_ref.at[mine], 5, d - 1, ydev[d]) for d in (2, 1, 3)]

    for copy in sums_za:
        copy.wait_recv()
    total = qa[at(z * ZA, ZA), :]
    for d in range(NZ - 1):
        total = total + r3a[d]
    mine = at(half + y * YA + z * ZA, ZA)
    o_ref[mine, :] = total
    back_za = [send(o_ref.at[mine], o_ref.at[mine], 6, d - 1, zdev[d]) for d in ZORDER]

    for copy in back_yb:
        copy.wait_recv()
    own = at(half + PA + z * ZB, ZB)
    back_zb = [send(o_ref.at[own], o_ref.at[own], 7, d - 1, zdev[d]) for d in ZORDER]
    for copy in back_za:
        copy.wait_recv()
    own = at(half + y * YA, YA)
    back_ya = [send(o_ref.at[own], o_ref.at[own], 8, d - 1, ydev[d]) for d in (2, 1, 3)]
    back = [send(o_ref.at[own], o_ref.at[own], 9, 0, other)]
    for copy in back_zb:
        copy.wait_recv()
    part = at(half + PA, PB)
    back.append(send(o_ref.at[part], o_ref.at[part], 9, 1, other))
    for n, d in enumerate((2, 1, 3)):
        back_ya[n].wait_recv()
        part = at(half + lax.rem(y + NY - d, NY) * YA, YA)
        back.append(send(o_ref.at[part], o_ref.at[part], 9, 2 + n, other))
    for copy in back:
        copy.wait_recv()
    for copy in sent:
        copy.wait_send()


def comm(g):
    counts = (5, 3, 7, 3, 7, 3, 7, 7, 3, 5)
    buffers = ((HALF,), (HALF,), (3, YA), (7, ZB), (YA,), (ZB,), (7, ZA), (3, YB))
    return pl.pallas_call(
        comm_kern,
        out_shape=jax.ShapeDtypeStruct((2 * HALF, 128), F32),
        in_specs=[pl.BlockSpec(memory_space=pltpu.VMEM)],
        out_specs=pl.BlockSpec(memory_space=pltpu.VMEM),
        scratch_shapes=[pltpu.VMEM(b + (128,), F32) for b in buffers]
        + [pltpu.SemaphoreType.DMA((n,)) for n in counts for _ in range(2)],
        compiler_params=pltpu.CompilerParams(
            vmem_limit_bytes=56 * 2**20, collective_id=0, has_side_effects=True),
        name="comm")(g)


def route_kern(plan_ref, t_ref):
    me = lax.axis_index("pair")

    def pick(values, n):
        out = values[0]
        for i in range(1, len(values)):
            out = jnp.where(n == i, values[i], out)
        return out

    def choose(firsts, seconds):
        best = jnp.int32(0)
        one = [jnp.left_shift(1, v) for v in firsts]
        two = [jnp.left_shift(1, v) for v in seconds]
        for mask in range(16):
            seen = 0
            for q in range(4):
                seen = seen | (two[q] if mask >> q & 1 else one[q])
            best = jnp.where(seen == 15, mask, best)
        return [jnp.right_shift(best, q) & 1 for q in range(4)]

    def number(perm):
        a, b, c, d = perm
        return 6 * a + 2 * (b - (a < b).astype(jnp.int32)) + (c > d).astype(jnp.int32)

    def invert(perm):
        return [sum(q * (perm[q] == v).astype(jnp.int32) for q in range(4)) for v in range(4)]

    first = [plan_ref[0, 2 * q] for q in range(4)]
    second = [plan_ref[0, 2 * q + 1] for q in range(4)]
    bit = choose([v >> 1 for v in first], [v >> 1 for v in second])
    kept = [jnp.where(bit[q] == 1, second[q], first[q]) for q in range(4)]
    moved = [jnp.where(bit[q] == 1, first[q], second[q]) for q in range(4)]
    home = [v >> 1 for v in kept]
    at = invert(home)
    source = [v >> 1 for v in moved]
    came = invert(source)
    t_ref[0] = number([pick(home, came[d]) for d in range(4)])
    mine = pick(at, me)
    t_ref[3] = pick(kept, mine) & 1
    t_ref[4] = pick(bit, mine)

    place = [sum(p * (plan_ref[1, p] == v).astype(jnp.int32) for p in range(8)) for v in range(8)]
    goes0 = [pick(place, pick(first, at[d])) for d in range(4)]
    goes1 = [pick(place, pick(second, at[d])) for d in range(4)]
    bit = choose([v >> 1 for v in goes0], [v >> 1 for v in goes1])
    early = [jnp.where(bit[d] == 1, goes1[d], goes0[d]) for d in range(4)]
    late = [jnp.where(bit[d] == 1, goes0[d], goes1[d]) for d in range(4)]
    t_ref[1] = number([v >> 1 for v in early])
    t_ref[2] = number([v >> 1 for v in late])
    t_ref[5] = pick(bit, me)
    t_ref[6] = pick(early, pick(invert([v >> 1 for v in early]), me)) & 1
    t_ref[7] = 0


def route(plan):
    return pl.pallas_call(
        route_kern,
        out_shape=jax.ShapeDtypeStruct((8,), jnp.int32),
        in_specs=[pl.BlockSpec(memory_space=pltpu.SMEM)],
        out_specs=pl.BlockSpec(memory_space=pltpu.SMEM),
        name="route")(plan)


PERMS = list(itertools.permutations(range(4)))


def permute(number, x):
    def move(perm):
        return lambda v: lax.ppermute(v, "pair", [(i, perm[i]) for i in range(4)])

    return lax.switch(number, [lambda v: v] + [move(perm) for perm in PERMS[1:]], x)


def body(matrix, plan):
    t = route(plan)
    keep, away = solve(t, comm(gram(t, (matrix,))), (matrix,), 3)
    parts = (keep, permute(t[0], away))
    early, late = solve(t, comm(gram(t, parts)), parts, 5)
    early = permute(t[1], early)
    late = permute(t[2], late)
    swap = t[6] == 1
    return jnp.concatenate([jnp.where(swap, late, early), jnp.where(swap, early, late)], axis=1)


def solution(mesh):
    placed = (P("row", "pair"), P())
    return jax.shard_map(
        body, mesh=mesh, in_specs=placed, out_specs=P("row", "pair"), check_vma=False
    )
```

```python
import functools
import itertools

import jax
import jax.numpy as jnp
from jax import lax
from jax.experimental import pallas as pl
from jax.experimental.pallas import tpu as pltpu
from jax.sharding import PartitionSpec as P

F32 = jnp.float32
BF = jnp.bfloat16
MESH = pl.DeviceIdType.MESH
OFF = [(i, j) for i in range(8) for j in range(i + 1, 8)]
NZ, NY = 8, 4
HALF, PA, PB = 2048, 1536, 512
YA, ZA, ZB, YB = PA // NY, PA // NY // NZ, PB // NZ, PB // NZ // NY
ZORDER = (4, 3, 5, 2, 6, 1, 7)


def split(x):
    hi = x.astype(BF)
    return hi, (x - hi.astype(F32)).astype(BF)


def dot(a, b):
    return jnp.dot(a, b, preferred_element_type=F32)


def iotas(n, m):
    shape = (n, m)
    return lax.broadcasted_iota(jnp.int32, shape, 0), lax.broadcasted_iota(jnp.int32, shape, 1)


def vmem_call(kern, outs, n_smem, scratch, name, *args):
    vm = pl.BlockSpec(memory_space=pltpu.VMEM)
    sm = pl.BlockSpec(memory_space=pltpu.SMEM)
    return pl.pallas_call(
        kern,
        out_shape=outs,
        in_specs=[sm] * n_smem + [vm] * (len(args) - n_smem),
        out_specs=jax.tree.map(lambda _: vm, outs),
        scratch_shapes=scratch,
        compiler_params=pltpu.CompilerParams(vmem_limit_bytes=32 * 2**20),
        name=name,
    )(*args)


def load_pair(t_ref, parts, dst, row0):
    if len(parts) == 1:
        dst[row0:row0 + 256, :] = parts[0][...]
        return
    at = t_ref[4] * 512
    dst[row0:row0 + 256, pl.ds(pl.multiple_of(at, 512), 512)] = parts[0][...]
    dst[row0:row0 + 256, pl.ds(pl.multiple_of(512 - at, 512), 512)] = parts[1][...]


def gram_kern(n_parts, t_ref, *refs):
    parts = refs[:n_parts]
    g_ref, x_ref, ph, plo, th, tl = refs[n_parts:]
    load_pair(t_ref, parts, x_ref, 0)
    for c in range(0, 1024, 256):
        x = x_ref[:, c:c + 256]
        ph[:, c:c + 256], plo[:, c:c + 256] = split(x)
        th[c:c + 256, :], tl[c:c + 256, :] = split(x.T)
    bi, bj = iotas(128, 128)
    for i in range(4):
        r = slice(256 * i, 256 * i + 256)
        for j in range(i, 4):
            c = slice(256 * j, 256 * j + 256)
            g = dot(th[r, :], ph[:, c]) + (dot(th[r, :], plo[:, c]) + dot(tl[r, :], ph[:, c]))
            for u in range(2):
                for v in range(2):
                    if (2 * i + u, 2 * j + v) in OFF:
                        n = 128 * OFF.index((2 * i + u, 2 * j + v))
                        g_ref[n:n + 128, :] = g[128 * u:128 * u + 128, 128 * v:128 * v + 128]
            if i == j:
                n = 128 * (28 + i)
                g_ref[n:n + 128, :] = jnp.where(bj > bi, g[:128, :128], g[128:, 128:])


def gram(t, parts):
    return vmem_call(
        functools.partial(gram_kern, len(parts)),
        jax.ShapeDtypeStruct((4096, 128), F32),
        1,
        [pltpu.VMEM((256, 1024), F32)] + [pltpu.VMEM((256, 1024), BF)] * 2 + [pltpu.VMEM((1024, 256), BF)] * 2,
        "gram", t, *parts)


def lane_bcast(x, c):
    return jnp.broadcast_to(x[:, c:c + 1], (8, 128))


def row_bcast(x, s):
    return jnp.broadcast_to(x[s:s + 1, :], (8, 128))


def total8(t):
    return ((t[0] + t[1]) + (t[2] + t[3])) + ((t[4] + t[5]) + (t[6] + t[7]))


def invert128(m, work):
    sub, lane = iotas(8, 128)
    m = list(m)
    for p in range(16):
        work(p)
        inside = (lane >= 8 * p) & (lane < 8 * p + 8)
        e = [lane_bcast(m[p], 8 * p + k) for k in range(8)]
        for s in range(0, 8, 2):
            u, v = e[s], e[s + 1]
            a, b, c, d = row_bcast(u, s), row_bcast(v, s), row_bcast(u, s + 1), row_bcast(v, s + 1)
            rd = 1.0 / (a * d - b * c)
            r0, r1 = sub == s, sub == s + 1
            new = list(e)
            for j in range(8):
                if j == s:
                    t0, t1, old = d * rd, -c * rd, 0.0
                elif j == s + 1:
                    t0, t1, old = -b * rd, a * rd, 0.0
                else:
                    x0, x1, old = row_bcast(e[j], s), row_bcast(e[j], s + 1), e[j]
                    t0, t1 = (d * x0 - b * x1) * rd, (a * x1 - c * x0) * rd
                new[j] = jnp.where(r0, t0, jnp.where(r1, t1, old - u * t0 - v * t1))
            e = new
        mp = jnp.where(inside, jnp.where(lane - 8 * p == sub, 1.0, 0.0), m[p])
        n = total8([e[k] * row_bcast(mp, k) for k in range(8)])
        nb = [row_bcast(n, k) for k in range(8)]
        for r in range(16):
            if r != p:
                t = total8([lane_bcast(m[r], 8 * p + k) * nb[k] for k in range(8)])
                m[r] = jnp.where(inside, 0.0, m[r]) - t
        m[p] = n
    return m


def solve_kern(n_parts, t_ref, g_ref, *refs):
    parts = refs[:n_parts]
    o_refs, (c_ref, x_ref, d_ref, w_ref, wh_ref, wl_ref, y_ref) = refs[n_parts:-7], refs[-7:]
    bi, bj = iotas(128, 128)
    dif = (bj - bi).astype(F32)
    eye = jnp.where(bi == bj, 1.0, 0.0)
    scale = 1.0 / (1024 * 128 * 2)
    for n, (i, j) in enumerate(OFF):
        k = g_ref[128 * n:128 * n + 128, :] * ((dif + 128.0 * (j - i)) * scale)
        c_ref[128 * i:128 * i + 128, 128 * j:128 * j + 128] = -k
        c_ref[128 * j:128 * j + 128, 128 * i:128 * i + 128] = k.T
    for m in range(4):
        k = g_ref[128 * (28 + m):128 * (29 + m), :] * (dif * scale)
        up = jnp.where(bj > bi, k, 0.0)
        low = jnp.where(bj < bi, k, 0.0)
        a = 256 * m
        c_ref[a:a + 128, a:a + 128] = eye - (up - up.T)
        c_ref[a + 128:a + 256, a + 128:a + 256] = eye - (low - low.T)
    load_pair(t_ref, parts, c_ref, 1024)
    for ref in (wh_ref, wl_ref, y_ref):
        ref[...] = jnp.zeros(ref.shape, BF)
    d_ref[...] = c_ref[0:128, 0:128]

    def update(r, cs):
        c_ref[r, cs] = c_ref[r, cs] - (dot(y_ref[r, :], wh_ref[:, cs]) + dot(y_ref[r, :], wl_ref[:, cs]))

    def work(p):
        update(slice(256 * (p // 4) + 256, 256 * (p // 4) + 512), slice(256 * (p % 4), 256 * (p % 4) + 256))

    def step(k, _):
        kc = pl.ds(pl.multiple_of(k * 128, 128), 128)
        m = invert128([d_ref[8 * r:8 * r + 8, :] for r in range(16)], work)
        for r in range(16):
            d_ref[8 * r:8 * r + 8, :] = m[r]
        c_ref[kc, kc] = jnp.zeros((128, 128), F32)
        dh, dl = split(d_ref[...])
        w_ref[0:128, 0:128] = dh
        w_ref[128:256, 0:128] = dh
        w_ref[0:128, 128:256] = dl
        w_ref[128:256, 128:256] = dl
        for c in range(0, 1024, 256):
            hi, lo = split(c_ref[kc, c:c + 256])
            wh_ref[0:128, c:c + 256] = hi
            wh_ref[128:256, c:c + 256] = hi
            wl_ref[0:128, c:c + 256] = lo
            wl_ref[128:256, c:c + 256] = lo

        def rows(i, _):
            r = pl.ds(pl.multiple_of(i * 256, 256), 256)
            y = dot(jnp.concatenate(split(c_ref[r, kc]), axis=1), w_ref[...])
            y = y[:, :128] + y[:, 128:]
            y_ref[r, :] = jnp.concatenate(split(y), axis=1)
            c_ref[r, kc] = y
            return 0

        lax.fori_loop((k + 1) // 2, 5, rows, 0)

        def first_rows(i, _):
            for c in range(0, 1024, 256):
                update(slice(0, 256), slice(c, c + 256))
            return 0

        lax.fori_loop(k, 1, first_rows, 0)
        nc = pl.ds(pl.multiple_of(jnp.minimum(k + 1, 7) * 128, 128), 128)
        gone = jnp.where(k == 0, 0.0, 1.0)
        y = y_ref[nc, :]
        d_ref[...] = c_ref[nc, nc] - gone * (dot(y, wh_ref[:, nc]) + dot(y, wl_ref[:, nc]))
        return 0

    lax.fori_loop(0, 8, step, 0)
    load_pair(t_ref, parts, x_ref, 0)
    for c in range(0, 1024, 256):
        update(slice(1024, 1280), slice(c, c + 256))
    if n_parts == 1:
        for o_ref, half in zip(o_refs, (t_ref[5], 1 - t_ref[5])):
            cs = pl.ds(pl.multiple_of(half * 512, 512), 512)
            o_ref[...] = 2.0 * c_ref[1024:1280, cs] - x_ref[:, cs]
    else:
        for n in range(2):
            cs = slice(512 * n, 512 * n + 512)
            o_refs[0][n] = 2.0 * c_ref[1024:1280, cs] - x_ref[:, cs]


def solve(t, g, parts):
    half = jax.ShapeDtypeStruct((256, 512), F32)
    return vmem_call(
        functools.partial(solve_kern, len(parts)),
        (half, half) if len(parts) == 1 else jax.ShapeDtypeStruct((2, 256, 512), F32),
        1,
        [pltpu.VMEM((1280, 1024), F32), pltpu.VMEM((256, 1024), F32), pltpu.VMEM((128, 128), F32),
         pltpu.VMEM((256, 256), BF)] + [pltpu.VMEM((256, 1024), BF)] * 2 + [pltpu.VMEM((1280, 256), BF)],
        "solve", t, g, *parts)


def comm_kern(g_ref, o_ref, r1, h, r2a, r2b, qa, qb, r3a, r3b, *sems):
    row = lax.axis_index("row")
    c = lax.rem(row, 2)
    y = lax.rem(row // 2, NY)
    z = row // (2 * NY)
    ys = [lax.rem(y + d, NY) for d in range(NY)]
    zs = [lax.rem(z + d, NZ) for d in range(NZ)]
    ydev = [{"row": (z * NY + ys[d]) * 2 + c} for d in range(NY)]
    zdev = [{"row": (zs[d] * NY + y) * 2 + c} for d in range(NZ)]
    other = {"row": (z * NY + y) * 2 + 1 - c}
    half = c * HALF

    def at(start, size):
        return pl.ds(pl.multiple_of(start, 8), size)

    barrier = pltpu.get_barrier_semaphore()
    for target in [other] + ydev[1:] + zdev[1:]:
        pl.semaphore_signal(barrier, inc=1, device_id=target, device_id_type=MESH)
    pl.semaphore_wait(barrier, NY + NZ - 1)

    sent = []

    def send(src, dst, pair, n, target):
        copy = pltpu.make_async_remote_copy(
            src_ref=src, dst_ref=dst, send_sem=sems[2 * pair].at[n], recv_sem=sems[2 * pair + 1].at[n],
            device_id=target, device_id_type=MESH)
        copy.start()
        sent.append(copy)
        return copy

    chunks = [at(ys[d] * YA, YA) for d in (1, 3, 2)] + [at(PA, PB), at(y * YA, YA)]
    core = [send(g_ref.at[at((1 - c) * HALF + s.start, s.size)], r1.at[s], 0, n, other) for n, s in enumerate(chunks)]

    def add(s):
        h[s, :] = g_ref[at(half + s.start, s.size), :] + r1[s, :]

    sums_ya, sums_zb = [], []
    for n, d in enumerate((1, 3, 2)):
        core[n].wait_recv()
        add(chunks[n])
        sums_ya.append(send(h.at[chunks[n]], r2a.at[d - 1], 1, d - 1, ydev[d]))
    core[3].wait_recv()
    for d in ZORDER:
        s = at(PA + zs[d] * ZB, ZB)
        add(s)
        sums_zb.append(send(h.at[s], r2b.at[d - 1], 2, d - 1, zdev[d]))
    add(at(PA + z * ZB, ZB))
    core[4].wait_recv()
    add(chunks[4])

    for copy in sums_zb:
        copy.wait_recv()
    total = h[at(PA + z * ZB, ZB), :]
    for d in range(NZ - 1):
        total = total + r2b[d]
    qb[...] = total
    sums_yb = [send(qb.at[at(ys[d] * YB, YB)], r3b.at[d - 1], 3, d - 1, ydev[d]) for d in (2, 1, 3)]

    for copy in sums_ya:
        copy.wait_recv()
    sums_za = []
    for d in ZORDER + (0,):
        s = at(zs[d] * ZA, ZA)
        qa[s, :] = (h[at(y * YA + zs[d] * ZA, ZA), :] + r2a[0, s, :]) + (r2a[1, s, :] + r2a[2, s, :])
        if d:
            sums_za.append(send(qa.at[s], r3a.at[d - 1], 4, d - 1, zdev[d]))

    for copy in sums_yb:
        copy.wait_recv()
    mine = at(half + PA + z * ZB + y * YB, YB)
    o_ref[mine, :] = (qb[at(y * YB, YB), :] + r3b[0]) + (r3b[1] + r3b[2])
    back_yb = [send(o_ref.at[mine], o_ref.at[mine], 5, d - 1, ydev[d]) for d in (2, 1, 3)]

    for copy in sums_za:
        copy.wait_recv()
    total = qa[at(z * ZA, ZA), :]
    for d in range(NZ - 1):
        total = total + r3a[d]
    mine = at(half + y * YA + z * ZA, ZA)
    o_ref[mine, :] = total
    back_za = [send(o_ref.at[mine], o_ref.at[mine], 6, d - 1, zdev[d]) for d in ZORDER]

    for copy in back_yb:
        copy.wait_recv()
    own = at(half + PA + z * ZB, ZB)
    back_zb = [send(o_ref.at[own], o_ref.at[own], 7, d - 1, zdev[d]) for d in ZORDER]
    for copy in back_za:
        copy.wait_recv()
    own = at(half + y * YA, YA)
    back_ya = [send(o_ref.at[own], o_ref.at[own], 8, d - 1, ydev[d]) for d in (2, 1, 3)]
    back = [send(o_ref.at[own], o_ref.at[own], 9, 0, other)]
    for copy in back_zb:
        copy.wait_recv()
    part = at(half + PA, PB)
    back.append(send(o_ref.at[part], o_ref.at[part], 9, 1, other))
    for n, d in enumerate((2, 1, 3)):
        back_ya[n].wait_recv()
        part = at(half + lax.rem(y + NY - d, NY) * YA, YA)
        back.append(send(o_ref.at[part], o_ref.at[part], 9, 2 + n, other))
    for copy in back:
        copy.wait_recv()
    for copy in sent:
        copy.wait_send()


def comm(g):
    counts = (5, 3, 7, 3, 7, 3, 7, 7, 3, 5)
    buffers = ((HALF,), (HALF,), (3, YA), (7, ZB), (YA,), (ZB,), (7, ZA), (3, YB))
    return pl.pallas_call(
        comm_kern,
        out_shape=jax.ShapeDtypeStruct((2 * HALF, 128), F32),
        in_specs=[pl.BlockSpec(memory_space=pltpu.VMEM)],
        out_specs=pl.BlockSpec(memory_space=pltpu.VMEM),
        scratch_shapes=[pltpu.VMEM(b + (128,), F32) for b in buffers]
        + [pltpu.SemaphoreType.DMA((n,)) for n in counts for _ in range(2)],
        compiler_params=pltpu.CompilerParams(
            vmem_limit_bytes=24 * 2**20, collective_id=0, has_side_effects=True),
        name="comm")(g)


def swap_kern(n_blocks, t_ref, x_ref, o_ref, mid, out, ss1, rs1, ss2, rs2):
    me = lax.axis_index("pair")
    others = [lax.rem(me + d, 4) for d in range(4)]
    barrier = pltpu.get_barrier_semaphore()
    for d in (2, 1, 3):
        pl.semaphore_signal(barrier, inc=1, device_id={"pair": others[d]}, device_id_type=MESH)
    pl.semaphore_wait(barrier, 3)

    def rows(j):
        return pl.ds(pl.multiple_of(64 * j, 64), 64)

    def send(src, dst, ss, rs, d):
        copy = pltpu.make_async_remote_copy(
            src_ref=src, dst_ref=dst, send_sem=ss.at[d - 1], recv_sem=rs.at[d - 1],
            device_id={"pair": others[d]}, device_id_type=MESH)
        copy.start()
        return copy

    there = [send(x_ref.at[:, rows(others[d]), :], mid.at[:, me], ss1, rs1, d) for d in (2, 1, 3)]
    mid[:, me] = x_ref[:, rows(me), :]
    for copy in there:
        copy.wait_recv()
    back = []
    for d in (2, 1, 3, 0):
        for n in range(n_blocks):
            at = t_ref[8 + n_blocks * others[d] + n] if n_blocks == 2 else t_ref[others[d]]
            block = mid[at // 4, at % 4]
            if d:
                out[d - 1, :, 512 * n:512 * n + 512] = block
            else:
                o_ref[rows(me), 512 * n:512 * n + 512] = block
        if d:
            back.append(send(out.at[d - 1], o_ref.at[rows(me), :], ss2, rs2, d))
    for copy in back:
        copy.wait_recv()
    for copy in there + back:
        copy.wait_send()


def swap(t, x):
    n = x.shape[0]
    vm = pl.BlockSpec(memory_space=pltpu.VMEM)
    return pl.pallas_call(
        functools.partial(swap_kern, n),
        out_shape=jax.ShapeDtypeStruct((256, 512 * n), F32),
        in_specs=[pl.BlockSpec(memory_space=pltpu.SMEM), vm],
        out_specs=vm,
        scratch_shapes=[pltpu.VMEM((n, 4, 64, 512), F32), pltpu.VMEM((3, 64, 512 * n), F32)]
        + [pltpu.SemaphoreType.DMA((3,))] * 4,
        compiler_params=pltpu.CompilerParams(
            vmem_limit_bytes=16 * 2**20, collective_id=n, has_side_effects=True),
        name="swap")(t, x)


def route_kern(plan_ref, t_ref):
    me = lax.axis_index("pair")

    def pick(values, n):
        out = values[0]
        for i in range(1, len(values)):
            out = jnp.where(n == i, values[i], out)
        return out

    def place(values, v):
        return sum(i * (x == v).astype(jnp.int32) for i, x in enumerate(values))

    first = [plan_ref[0, 2 * q] for q in range(4)]
    second = [plan_ref[0, 2 * q + 1] for q in range(4)]
    one = [jnp.left_shift(1, v >> 1) for v in first]
    two = [jnp.left_shift(1, v >> 1) for v in second]
    best = jnp.int32(0)
    for mask in range(16):
        seen = 0
        for q in range(4):
            seen = seen | (two[q] if mask >> q & 1 else one[q])
        best = jnp.where(seen == 15, mask, best)
    bit = [jnp.right_shift(best, q) & 1 for q in range(4)]
    kept = [jnp.where(bit[q] == 1, second[q], first[q]) for q in range(4)]
    moved = [jnp.where(bit[q] == 1, first[q], second[q]) for q in range(4)]
    home = [v >> 1 for v in kept]
    for d in range(4):
        t_ref[d] = pick(moved, place(home, d)) >> 1
    mine = place(home, me)
    t_ref[4] = pick(bit, mine)
    t_ref[5] = pick(kept, mine) & 1
    t_ref[6] = 0
    t_ref[7] = 0
    where = [4 * (i % 2) + home[i // 2] for i in range(8)]
    blocks = [plan_ref[0, i] for i in range(8)]
    for p in range(8):
        t_ref[8 + p] = pick(where, place(blocks, plan_ref[1, p]))


def route(plan):
    return pl.pallas_call(
        route_kern,
        out_shape=jax.ShapeDtypeStruct((16,), jnp.int32),
        in_specs=[pl.BlockSpec(memory_space=pltpu.SMEM)],
        out_specs=pl.BlockSpec(memory_space=pltpu.SMEM),
        name="route")(plan)


def body(matrix, plan):
    t = route(plan)
    keep, away = solve(t, comm(gram(t, (matrix,))), (matrix,))
    parts = (keep, swap(t, away[None]))
    return swap(t, solve(t, comm(gram(t, parts)), parts))


def solution(mesh):
    placed = (P("row", "pair"), P())
    return jax.shard_map(
        body, mesh=mesh, in_specs=placed, out_specs=P("row", "pair"), check_vma=False
    )
```

```python
import functools
import itertools

import jax
import jax.numpy as jnp
from jax import lax
from jax.experimental import pallas as pl
from jax.experimental.pallas import tpu as pltpu
from jax.sharding import PartitionSpec as P

F32 = jnp.float32
BF = jnp.bfloat16
MESH = pl.DeviceIdType.MESH
OFF = [(i, j) for i in range(8) for j in range(i + 1, 8)]
NZ, NY = 8, 4
HALF, PA, PB = 2048, 1280, 768
YA, ZA, ZB, YB = PA // NY, PA // NY // NZ, PB // NZ, PB // NZ // NY
ZORDER = (4, 3, 5, 2, 6, 1, 7)


def split(x):
    hi = x.astype(BF)
    return hi, (x - hi.astype(F32)).astype(BF)


def dot(a, b):
    return jnp.dot(a, b, preferred_element_type=F32)


def iotas(n, m):
    shape = (n, m)
    return lax.broadcasted_iota(jnp.int32, shape, 0), lax.broadcasted_iota(jnp.int32, shape, 1)


def vmem_call(kern, outs, n_smem, scratch, name, *args):
    vm = pl.BlockSpec(memory_space=pltpu.VMEM)
    sm = pl.BlockSpec(memory_space=pltpu.SMEM)
    return pl.pallas_call(
        kern,
        out_shape=outs,
        in_specs=[sm] * n_smem + [vm] * (len(args) - n_smem),
        out_specs=jax.tree.map(lambda out: sm if out.dtype == jnp.int32 else vm, outs),
        scratch_shapes=scratch,
        compiler_params=pltpu.CompilerParams(vmem_limit_bytes=32 * 2**20),
        name=name,
    )(*args)


def load_pair(t_ref, parts, dst, row0):
    if len(parts) == 1:
        dst[row0:row0 + 256, :] = parts[0][...]
        return
    at = t_ref[4] * 512
    dst[row0:row0 + 256, pl.ds(pl.multiple_of(at, 512), 512)] = parts[0][...]
    dst[row0:row0 + 256, pl.ds(pl.multiple_of(512 - at, 512), 512)] = parts[1][...]


def gram_kern(n_parts, t_ref, *refs):
    parts = refs[:n_parts]
    if n_parts == 1:
        g_ref, table_ref, x_ref, ph, plo, th, tl = refs[n_parts:]
        route(t_ref, table_ref)
    else:
        g_ref, x_ref, ph, plo, th, tl = refs[n_parts:]
    load_pair(t_ref, parts, x_ref, 0)
    for c in range(0, 1024, 256):
        x = x_ref[:, c:c + 256]
        ph[:, c:c + 256], plo[:, c:c + 256] = split(x)
        th[c:c + 256, :], tl[c:c + 256, :] = split(x.T)
    bi, bj = iotas(128, 128)
    for i in range(4):
        r = slice(256 * i, 256 * i + 256)
        for j in range(i, 4):
            c = slice(256 * j, 256 * j + 256)
            g = dot(th[r, :], ph[:, c]) + (dot(th[r, :], plo[:, c]) + dot(tl[r, :], ph[:, c]))
            for u in range(2):
                for v in range(2):
                    if (2 * i + u, 2 * j + v) in OFF:
                        n = 128 * OFF.index((2 * i + u, 2 * j + v))
                        g_ref[n:n + 128, :] = g[128 * u:128 * u + 128, 128 * v:128 * v + 128]
            if i == j:
                n = 128 * (28 + i)
                g_ref[n:n + 128, :] = jnp.where(bj > bi, g[:128, :128], g[128:, 128:])


def gram(t, parts):
    out = jax.ShapeDtypeStruct((4096, 128), F32)
    return vmem_call(
        functools.partial(gram_kern, len(parts)),
        (out, jax.ShapeDtypeStruct((16,), jnp.int32)) if len(parts) == 1 else out,
        1,
        [pltpu.VMEM((256, 1024), F32)] + [pltpu.VMEM((256, 1024), BF)] * 2 + [pltpu.VMEM((1024, 256), BF)] * 2,
        "gram", t, *parts)


def lane_bcast(x, c):
    return jnp.broadcast_to(x[:, c:c + 1], (8, 128))


def row_bcast(x, s):
    return jnp.broadcast_to(x[s:s + 1, :], (8, 128))


def total8(t):
    return ((t[0] + t[1]) + (t[2] + t[3])) + ((t[4] + t[5]) + (t[6] + t[7]))


def panel_product(m, n, p):
    x0, x1 = split(jnp.concatenate(m, axis=0))
    zero = [jnp.zeros((8, 128), F32)]
    y0, y1 = split(jnp.concatenate(zero * p + [n] + zero * (15 - p), axis=0))
    top = jnp.concatenate([y0, y1], axis=1)
    u = dot(jnp.concatenate([x0, x1], axis=1), jnp.concatenate([top, top], axis=0))
    return u[:, :128] + u[:, 128:]


def invert128(m, work):
    sub, lane = iotas(8, 128)
    m = list(m)
    e = [lane_bcast(m[0], k) for k in range(8)]
    for p in range(16):
        nxt = (p + 1) % 16
        left = [lane_bcast(m[nxt], 8 * p + k) for k in range(8)]
        work(p)
        upper = [lane_bcast(m[p], 8 * p + 8 + k) for k in range(8 if p < 15 else 0)]
        corner = [lane_bcast(m[nxt], 8 * p + 8 + k) for k in range(8 if p < 15 else 0)]
        after = (p + 2) % 16
        left2 = [lane_bcast(m[after], 8 * p + k) for k in range(8)]
        inside = (lane >= 8 * p) & (lane < 8 * p + 8)
        for s in range(0, 8, 2):
            u, v = e[s], e[s + 1]
            a, b, c, d = row_bcast(u, s), row_bcast(v, s), row_bcast(u, s + 1), row_bcast(v, s + 1)
            rd = 1.0 / (a * d - b * c)
            a, b, c, d = a * rd, b * rd, c * rd, d * rd
            r0, r1 = sub == s, sub == s + 1
            both = (sub >= s) & (sub <= s + 1)
            u, v = jnp.where(both, jnp.where(r0, -1.0, 0.0), u), jnp.where(both, jnp.where(r1, -1.0, 0.0), v)
            new = list(e)
            for j in range(8):
                if j == s:
                    new[j] = v * c - u * d
                elif j == s + 1:
                    new[j] = u * b - v * a
                else:
                    x0, x1 = row_bcast(e[j], s), row_bcast(e[j], s + 1)
                    new[j] = jnp.where(both, 0.0, e[j]) - u * (d * x0 - b * x1) - v * (a * x1 - c * x0)
            e = new
        ahead = []
        for k in range(len(corner)):
            x = total8([e[i] * row_bcast(upper[k], i) for i in range(8)])
            ahead.append(corner[k] - total8([left[i] * row_bcast(x, i) for i in range(8)]))
        mp = jnp.where(inside, jnp.where(lane - 8 * p == sub, 1.0, 0.0), m[p])
        n = total8([e[k] * row_bcast(mp, k) for k in range(8)])
        soon = jnp.where(inside, 0.0, m[nxt]) - total8([left[k] * row_bcast(n, k) for k in range(8)])
        soon2 = jnp.where(inside, 0.0, m[after]) - total8([left2[k] * row_bcast(n, k) for k in range(8)])
        e = ahead
        t = panel_product(m, n, p)
        for r in range(16):
            m[r] = n if r == p else soon if r == nxt else soon2 if r == after else jnp.where(inside, 0.0, m[r]) - t[8 * r:8 * r + 8, :]
    return m


def solve_kern(n_parts, t_ref, g_ref, *refs):
    parts = refs[:n_parts]
    o_refs, (c_ref, x_ref, d_ref, w_ref, a_ref, y_ref) = refs[n_parts:-6], refs[-6:]
    bi, bj = iotas(128, 128)
    dif = (bj - bi).astype(F32)
    eye = jnp.where(bi == bj, 1.0, 0.0)
    scale = 1.0 / (1024 * 128 * 2)
    for n, (i, j) in enumerate(OFF):
        k = g_ref[128 * n:128 * n + 128, :] * ((dif + 128.0 * (j - i)) * scale)
        c_ref[128 * i:128 * i + 128, 128 * j:128 * j + 128] = -k
        c_ref[128 * j:128 * j + 128, 128 * i:128 * i + 128] = k.T
    for m in range(4):
        k = g_ref[128 * (28 + m):128 * (29 + m), :] * (dif * scale)
        up = jnp.where(bj > bi, k, 0.0)
        low = jnp.where(bj < bi, k, 0.0)
        a = 256 * m
        c_ref[a:a + 128, a:a + 128] = eye - (up - up.T)
        c_ref[a + 128:a + 256, a + 128:a + 256] = eye - (low - low.T)
    load_pair(t_ref, parts, c_ref, 1024)
    for ref in (w_ref, y_ref):
        ref[...] = jnp.zeros(ref.shape, BF)
    d_ref[...] = c_ref[0:128, 0:128]

    def columns(k):
        return pl.ds(pl.multiple_of(k * 128, 128), 128)

    def scaled(r, kc):
        y = dot(jnp.concatenate(split(c_ref[r, kc]), axis=1), w_ref[...])
        y = y[:, :128] + y[:, 128:]
        return y, jnp.concatenate(split(y) * 2, axis=1)

    def pivot_rows(kc, cs):
        hi, lo = split(c_ref[kc, cs])
        for i, x in enumerate((hi, hi, lo, lo)):
            a_ref[128 * i:128 * i + 128, cs] = x

    def update(r, cs):
        c_ref[r, cs] = c_ref[r, cs] - dot(y_ref[r, :], a_ref[:, cs])

    def step(first, k, _):
        before = columns(jnp.maximum(k - 1, 0))

        def work(p):
            each = 4 * (5 - first)
            if p * each % 16 >= each:
                return
            p = p * each // 16
            r = slice(256 * (p // 4 + first), 256 * (p // 4 + first) + 256)
            cs = slice(256 * (p % 4), 256 * (p % 4) + 256)
            if p < 4:
                pivot_rows(before, cs)
            if p % 4 == 0:
                y, y_ref[r, :] = scaled(r, before)
                c_ref[r, before] = jnp.where(k == 0, c_ref[r, before], y)
            update(r, cs)

        m = invert128([d_ref[8 * r:8 * r + 8, :] for r in range(16)], work)
        for r in range(16):
            d_ref[8 * r:8 * r + 8, :] = m[r]
        kc = columns(k)
        c_ref[kc, kc] = jnp.zeros((128, 128), F32)
        dh, dl = split(d_ref[...])
        w_ref[0:128, 0:128] = dh
        w_ref[128:256, 0:128] = dh
        w_ref[0:128, 128:256] = dl
        w_ref[128:256, 128:256] = dl
        nc = columns(jnp.minimum(k + 1, 7))
        hi, lo = split(c_ref[kc, nc])
        _, y = scaled(nc, kc)
        d_ref[...] = c_ref[nc, nc] - dot(y, jnp.concatenate([hi, hi, lo, lo], axis=0))

        def first_rows(i, _):
            r = slice(0, 256)
            y, y_ref[r, :] = scaled(r, kc)
            c_ref[r, kc] = y
            for c in range(0, 1024, 256):
                pivot_rows(kc, slice(c, c + 256))
                update(r, slice(c, c + 256))
            return 0

        lax.fori_loop(k, 1, first_rows, 0)
        return 0

    for first, start, stop in ((1, 0, 4), (2, 4, 6), (3, 6, 8)):
        lax.fori_loop(start, stop, functools.partial(step, first), 0)
    last = slice(896, 1024)
    y, y_ref[1024:1280, :] = scaled(slice(1024, 1280), last)
    c_ref[1024:1280, last] = y
    for c in range(0, 1024, 256):
        pivot_rows(last, slice(c, c + 256))
        update(slice(1024, 1280), slice(c, c + 256))
    load_pair(t_ref, parts, x_ref, 0)
    if n_parts == 1:
        for o_ref, half in zip(o_refs, (t_ref[5], 1 - t_ref[5])):
            cs = pl.ds(pl.multiple_of(half * 512, 512), 512)
            o_ref[...] = 2.0 * c_ref[1024:1280, cs] - x_ref[:, cs]
    else:
        for n in range(2):
            cs = slice(512 * n, 512 * n + 512)
            o_refs[0][n] = 2.0 * c_ref[1024:1280, cs] - x_ref[:, cs]


def solve(t, g, parts):
    half = jax.ShapeDtypeStruct((256, 512), F32)
    return vmem_call(
        functools.partial(solve_kern, len(parts)),
        (half, half) if len(parts) == 1 else jax.ShapeDtypeStruct((2, 256, 512), F32),
        1,
        [pltpu.VMEM((1280, 1024), F32), pltpu.VMEM((256, 1024), F32), pltpu.VMEM((128, 128), F32),
         pltpu.VMEM((256, 256), BF)] + [pltpu.VMEM((512, 1024), BF), pltpu.VMEM((1280, 512), BF)],
        "solve", t, g, *parts)


def comm_kern(g_ref, o_ref, r1, h, r2a, r2b, qa, qb, r3a, r3b, *sems):
    row = lax.axis_index("row")
    c = lax.rem(row, 2)
    y = lax.rem(row // 2, NY)
    z = row // (2 * NY)
    ys = [lax.rem(y + d, NY) for d in range(NY)]
    zs = [lax.rem(z + d, NZ) for d in range(NZ)]
    ydev = [{"row": (z * NY + ys[d]) * 2 + c} for d in range(NY)]
    zdev = [{"row": (zs[d] * NY + y) * 2 + c} for d in range(NZ)]
    other = {"row": (z * NY + y) * 2 + 1 - c}
    half = c * HALF

    def at(start, size):
        return pl.ds(pl.multiple_of(start, 8), size)

    barrier = pltpu.get_barrier_semaphore()
    for target in [other] + ydev[1:] + zdev[1:]:
        pl.semaphore_signal(barrier, inc=1, device_id=target, device_id_type=MESH)
    pl.semaphore_wait(barrier, NY + NZ - 1)

    sent = []

    def send(src, dst, pair, n, target):
        copy = pltpu.make_async_remote_copy(
            src_ref=src, dst_ref=dst, send_sem=sems[2 * pair].at[n], recv_sem=sems[2 * pair + 1].at[n],
            device_id=target, device_id_type=MESH)
        copy.start()
        sent.append(copy)
        return copy

    chunks = [at(ys[d] * YA, YA) for d in (1, 3, 2)] + [at(PA, PB), at(y * YA, YA)]
    core = [send(g_ref.at[at((1 - c) * HALF + s.start, s.size)], r1.at[s], 0, n, other) for n, s in enumerate(chunks)]

    def add(s):
        h[s, :] = g_ref[at(half + s.start, s.size), :] + r1[s, :]

    sums_ya, sums_zb = [], []
    for n, d in enumerate((1, 3, 2)):
        core[n].wait_recv()
        add(chunks[n])
        sums_ya.append(send(h.at[chunks[n]], r2a.at[d - 1], 1, d - 1, ydev[d]))
    core[3].wait_recv()
    for d in ZORDER:
        s = at(PA + zs[d] * ZB, ZB)
        add(s)
        sums_zb.append(send(h.at[s], r2b.at[d - 1], 2, d - 1, zdev[d]))
    add(at(PA + z * ZB, ZB))
    core[4].wait_recv()
    add(chunks[4])

    for copy in sums_zb:
        copy.wait_recv()
    total = h[at(PA + z * ZB, ZB), :]
    for d in range(NZ - 1):
        total = total + r2b[d]
    qb[...] = total
    sums_yb = [send(qb.at[at(ys[d] * YB, YB)], r3b.at[d - 1], 3, d - 1, ydev[d]) for d in (2, 1, 3)]

    for copy in sums_ya:
        copy.wait_recv()
    sums_za = []
    for d in ZORDER + (0,):
        s = at(zs[d] * ZA, ZA)
        qa[s, :] = (h[at(y * YA + zs[d] * ZA, ZA), :] + r2a[0, s, :]) + (r2a[1, s, :] + r2a[2, s, :])
        if d:
            sums_za.append(send(qa.at[s], r3a.at[d - 1], 4, d - 1, zdev[d]))

    for copy in sums_yb:
        copy.wait_recv()
    mine = at(half + PA + z * ZB + y * YB, YB)
    o_ref[mine, :] = (qb[at(y * YB, YB), :] + r3b[0]) + (r3b[1] + r3b[2])
    back_yb = [send(o_ref.at[mine], o_ref.at[mine], 5, d - 1, ydev[d]) for d in (2, 1, 3)]

    for copy in sums_za:
        copy.wait_recv()
    total = qa[at(z * ZA, ZA), :]
    for d in range(NZ - 1):
        total = total + r3a[d]
    mine = at(half + y * YA + z * ZA, ZA)
    o_ref[mine, :] = total
    back_za = [send(o_ref.at[mine], o_ref.at[mine], 6, d - 1, zdev[d]) for d in ZORDER]

    for copy in back_yb:
        copy.wait_recv()
    own = at(half + PA + z * ZB, ZB)
    back_zb = [send(o_ref.at[own], o_ref.at[own], 7, d - 1, zdev[d]) for d in ZORDER]
    for copy in back_za:
        copy.wait_recv()
    own = at(half + y * YA, YA)
    back_ya = [send(o_ref.at[own], o_ref.at[own], 8, d - 1, ydev[d]) for d in (2, 1, 3)]
    back = [send(o_ref.at[own], o_ref.at[own], 9, 0, other)]
    for copy in back_zb:
        copy.wait_recv()
    part = at(half + PA, PB)
    back.append(send(o_ref.at[part], o_ref.at[part], 9, 1, other))
    for n, d in enumerate((2, 1, 3)):
        back_ya[n].wait_recv()
        part = at(half + lax.rem(y + NY - d, NY) * YA, YA)
        back.append(send(o_ref.at[part], o_ref.at[part], 9, 2 + n, other))
    for copy in back:
        copy.wait_recv()
    for copy in sent:
        copy.wait_send()


def comm(g):
    counts = (5, 3, 7, 3, 7, 3, 7, 7, 3, 5)
    buffers = ((HALF,), (HALF,), (3, YA), (7, ZB), (YA,), (ZB,), (7, ZA), (3, YB))
    return pl.pallas_call(
        comm_kern,
        out_shape=jax.ShapeDtypeStruct((2 * HALF, 128), F32),
        in_specs=[pl.BlockSpec(memory_space=pltpu.VMEM)],
        out_specs=pl.BlockSpec(memory_space=pltpu.VMEM),
        scratch_shapes=[pltpu.VMEM(b + (128,), F32) for b in buffers]
        + [pltpu.SemaphoreType.DMA((n,)) for n in counts for _ in range(2)],
        compiler_params=pltpu.CompilerParams(
            vmem_limit_bytes=24 * 2**20, collective_id=0, has_side_effects=True),
        name="comm")(g)


def swap_kern(n_blocks, t_ref, x_ref, o_ref, mid, out, ss1, rs1, ss2, rs2):
    me = lax.axis_index("pair")
    others = [lax.rem(me + d, 4) for d in range(4)]
    barrier = pltpu.get_barrier_semaphore()
    for d in (2, 1, 3):
        pl.semaphore_signal(barrier, inc=1, device_id={"pair": others[d]}, device_id_type=MESH)
    pl.semaphore_wait(barrier, 3)

    def rows(j):
        return pl.ds(pl.multiple_of(64 * j, 64), 64)

    def send(src, dst, ss, rs, d):
        copy = pltpu.make_async_remote_copy(
            src_ref=src, dst_ref=dst, send_sem=ss.at[d - 1], recv_sem=rs.at[d - 1],
            device_id={"pair": others[d]}, device_id_type=MESH)
        copy.start()
        return copy

    there = [send(x_ref.at[:, rows(others[d]), :], mid.at[:, me], ss1, rs1, d) for d in (2, 1, 3)]
    mid[:, me] = x_ref[:, rows(me), :]
    for copy in there:
        copy.wait_recv()
    back = []
    for d in (2, 1, 3, 0):
        for n in range(n_blocks):
            at = t_ref[8 + n_blocks * others[d] + n] if n_blocks == 2 else t_ref[others[d]]
            block = mid[at // 4, at % 4]
            if d:
                out[d - 1, :, 512 * n:512 * n + 512] = block
            else:
                o_ref[rows(me), 512 * n:512 * n + 512] = block
        if d:
            back.append(send(out.at[d - 1], o_ref.at[rows(me), :], ss2, rs2, d))
    for copy in back:
        copy.wait_recv()
    for copy in there + back:
        copy.wait_send()


def swap(t, x):
    n = x.shape[0]
    vm = pl.BlockSpec(memory_space=pltpu.VMEM)
    return pl.pallas_call(
        functools.partial(swap_kern, n),
        out_shape=jax.ShapeDtypeStruct((256, 512 * n), F32),
        in_specs=[pl.BlockSpec(memory_space=pltpu.SMEM), vm],
        out_specs=vm,
        scratch_shapes=[pltpu.VMEM((n, 4, 64, 512), F32), pltpu.VMEM((3, 64, 512 * n), F32)]
        + [pltpu.SemaphoreType.DMA((3,))] * 4,
        compiler_params=pltpu.CompilerParams(
            vmem_limit_bytes=16 * 2**20, collective_id=n, has_side_effects=True),
        name="swap")(t, x)


def route(plan_ref, t_ref):
    me = lax.axis_index("pair")

    def pick(values, n):
        out = values[0]
        for i in range(1, len(values)):
            out = jnp.where(n == i, values[i], out)
        return out

    def place(values, v):
        return sum(i * (x == v).astype(jnp.int32) for i, x in enumerate(values))

    first = [plan_ref[0, 2 * q] for q in range(4)]
    second = [plan_ref[0, 2 * q + 1] for q in range(4)]
    one = [jnp.left_shift(1, v >> 1) for v in first]
    two = [jnp.left_shift(1, v >> 1) for v in second]
    best = jnp.int32(0)
    for mask in range(16):
        seen = 0
        for q in range(4):
            seen = seen | (two[q] if mask >> q & 1 else one[q])
        best = jnp.where(seen == 15, mask, best)
    bit = [jnp.right_shift(best, q) & 1 for q in range(4)]
    kept = [jnp.where(bit[q] == 1, second[q], first[q]) for q in range(4)]
    moved = [jnp.where(bit[q] == 1, first[q], second[q]) for q in range(4)]
    home = [v >> 1 for v in kept]
    for d in range(4):
        t_ref[d] = pick(moved, place(home, d)) >> 1
    mine = place(home, me)
    t_ref[4] = pick(bit, mine)
    t_ref[5] = pick(kept, mine) & 1
    t_ref[6] = 0
    t_ref[7] = 0
    where = [4 * (i % 2) + home[i // 2] for i in range(8)]
    blocks = [plan_ref[0, i] for i in range(8)]
    for p in range(8):
        t_ref[8 + p] = pick(where, place(blocks, plan_ref[1, p]))


def body(matrix, plan):
    g, t = gram(plan, (matrix,))
    keep, away = solve(t, comm(g), (matrix,))
    parts = (keep, swap(t, away[None]))
    return swap(t, solve(t, comm(gram(t, parts)), parts))


def solution(mesh):
    placed = (P("row", "pair"), P())
    return jax.shard_map(
        body, mesh=mesh, in_specs=placed, out_specs=P("row", "pair"), check_vma=False
    )
```

```python
import functools
import itertools

import jax
import jax.numpy as jnp
from jax import lax
from jax.experimental import pallas as pl
from jax.experimental.pallas import tpu as pltpu
from jax.sharding import PartitionSpec as P

F32 = jnp.float32
BF = jnp.bfloat16
MESH = pl.DeviceIdType.MESH
OFF = [(i, j) for i in range(8) for j in range(i + 1, 8)]
NZ, NY = 8, 4
NA, HALF, PA, PB = 2, 2048, 768, 512
YA, ZA, ZB, YB = PA // NY, PA // NY // NZ, PB // NZ, PB // NZ // NY
YORDER = (2, 1, 3)
ZORDER = (4, 3, 5, 2, 6, 1, 7)
NS = 2


def split(x):
    hi = x.astype(BF)
    return hi, (x - hi.astype(F32)).astype(BF)


def dot(a, b):
    return jnp.dot(a, b, preferred_element_type=F32)


def iotas(n, m):
    shape = (n, m)
    return lax.broadcasted_iota(jnp.int32, shape, 0), lax.broadcasted_iota(jnp.int32, shape, 1)


def vmem_call(kern, outs, n_smem, scratch, name, *args):
    vm = pl.BlockSpec(memory_space=pltpu.VMEM)
    sm = pl.BlockSpec(memory_space=pltpu.SMEM)
    return pl.pallas_call(
        kern,
        out_shape=outs,
        in_specs=[sm] * n_smem + [vm] * (len(args) - n_smem),
        out_specs=jax.tree.map(lambda out: sm if out.dtype == jnp.int32 else vm, outs),
        scratch_shapes=scratch,
        compiler_params=pltpu.CompilerParams(vmem_limit_bytes=32 * 2**20),
        name=name,
    )(*args)


def load_pair(t_ref, parts, dst, row0):
    if len(parts) == 1:
        dst[row0:row0 + 256, :] = parts[0][...]
        return
    at = t_ref[4] * 512
    dst[row0:row0 + 256, pl.ds(pl.multiple_of(at, 512), 512)] = parts[0][...]
    dst[row0:row0 + 256, pl.ds(pl.multiple_of(512 - at, 512), 512)] = parts[1][...]


def gram_kern(n_parts, t_ref, *refs):
    parts = refs[:n_parts]
    if n_parts == 1:
        g_ref, table_ref, x_ref, ph, plo, th, tl = refs[n_parts:]
        route(t_ref, table_ref)
    else:
        g_ref, x_ref, ph, plo, th, tl = refs[n_parts:]
    load_pair(t_ref, parts, x_ref, 0)
    for c in range(0, 1024, 256):
        x = x_ref[:, c:c + 256]
        ph[:, c:c + 256], plo[:, c:c + 256] = split(x)
        th[c:c + 256, :], tl[c:c + 256, :] = split(x.T)
    bi, bj = iotas(128, 128)
    for i in range(4):
        r = slice(256 * i, 256 * i + 256)
        for j in range(i, 4):
            c = slice(256 * j, 256 * j + 256)
            g = dot(th[r, :], ph[:, c]) + (dot(th[r, :], plo[:, c]) + dot(tl[r, :], ph[:, c]))
            for u in range(2):
                for v in range(2):
                    if (2 * i + u, 2 * j + v) in OFF:
                        n = 128 * OFF.index((2 * i + u, 2 * j + v))
                        g_ref[n:n + 128, :] = g[128 * u:128 * u + 128, 128 * v:128 * v + 128]
            if i == j:
                n = 128 * (28 + i)
                g_ref[n:n + 128, :] = jnp.where(bj > bi, g[:128, :128], g[128:, 128:])


def gram(t, parts):
    out = jax.ShapeDtypeStruct((4096, 128), F32)
    return vmem_call(
        functools.partial(gram_kern, len(parts)),
        (out, jax.ShapeDtypeStruct((16,), jnp.int32)) if len(parts) == 1 else out,
        1,
        [pltpu.VMEM((256, 1024), F32)] + [pltpu.VMEM((256, 1024), BF)] * 2 + [pltpu.VMEM((1024, 256), BF)] * 2,
        "gram", t, *parts)


def lane_bcast(x, c):
    return jnp.broadcast_to(x[:, c:c + 1], (8, 128))


def row_bcast(x, s):
    return jnp.broadcast_to(x[s:s + 1, :], (8, 128))


def total8(t):
    return ((t[0] + t[1]) + (t[2] + t[3])) + ((t[4] + t[5]) + (t[6] + t[7]))


def panel_product(m, n, p):
    x0, x1 = split(jnp.concatenate(m, axis=0))
    zero = [jnp.zeros((8, 128), F32)]
    y0, y1 = split(jnp.concatenate(zero * p + [n] + zero * (15 - p), axis=0))
    top = jnp.concatenate([y0, y1], axis=1)
    u = dot(jnp.concatenate([x0, x1], axis=1), jnp.concatenate([top, top], axis=0))
    return u[:, :128] + u[:, 128:]


def invert128(m, work):
    sub, lane = iotas(8, 128)
    m = list(m)
    e = [lane_bcast(m[0], k) for k in range(8)]
    for p in range(16):
        nxt = (p + 1) % 16
        left = [lane_bcast(m[nxt], 8 * p + k) for k in range(8)]
        work(p)
        upper = [lane_bcast(m[p], 8 * p + 8 + k) for k in range(8 if p < 15 else 0)]
        corner = [lane_bcast(m[nxt], 8 * p + 8 + k) for k in range(8 if p < 15 else 0)]
        after = (p + 2) % 16
        left2 = [lane_bcast(m[after], 8 * p + k) for k in range(8)]
        inside = (lane >= 8 * p) & (lane < 8 * p + 8)
        for s in range(0, 8, 2):
            u, v = e[s], e[s + 1]
            a, b, c, d = row_bcast(u, s), row_bcast(v, s), row_bcast(u, s + 1), row_bcast(v, s + 1)
            rd = 1.0 / (a * d - b * c)
            a, b, c, d = a * rd, b * rd, c * rd, d * rd
            r0, r1 = sub == s, sub == s + 1
            both = (sub >= s) & (sub <= s + 1)
            u, v = jnp.where(both, jnp.where(r0, -1.0, 0.0), u), jnp.where(both, jnp.where(r1, -1.0, 0.0), v)
            new = list(e)
            for j in range(8):
                if j == s:
                    new[j] = v * c - u * d
                elif j == s + 1:
                    new[j] = u * b - v * a
                else:
                    x0, x1 = row_bcast(e[j], s), row_bcast(e[j], s + 1)
                    new[j] = jnp.where(both, 0.0, e[j]) - u * (d * x0 - b * x1) - v * (a * x1 - c * x0)
            e = new
        ahead = []
        for k in range(len(corner)):
            x = total8([e[i] * row_bcast(upper[k], i) for i in range(8)])
            ahead.append(corner[k] - total8([left[i] * row_bcast(x, i) for i in range(8)]))
        mp = jnp.where(inside, jnp.where(lane - 8 * p == sub, 1.0, 0.0), m[p])
        n = total8([e[k] * row_bcast(mp, k) for k in range(8)])
        soon = jnp.where(inside, 0.0, m[nxt]) - total8([left[k] * row_bcast(n, k) for k in range(8)])
        soon2 = jnp.where(inside, 0.0, m[after]) - total8([left2[k] * row_bcast(n, k) for k in range(8)])
        e = ahead
        t = panel_product(m, n, p)
        for r in range(16):
            m[r] = n if r == p else soon if r == nxt else soon2 if r == after else jnp.where(inside, 0.0, m[r]) - t[8 * r:8 * r + 8, :]
    return m


def solve_kern(n_parts, t_ref, g_ref, *refs):
    parts = refs[:n_parts]
    o_refs, (c_ref, x_ref, d_ref, w_ref, a_ref, y_ref) = refs[n_parts:-6], refs[-6:]
    bi, bj = iotas(128, 128)
    dif = (bj - bi).astype(F32)
    eye = jnp.where(bi == bj, 1.0, 0.0)
    scale = 1.0 / (1024 * 128 * 2)
    for n, (i, j) in enumerate(OFF):
        k = g_ref[128 * n:128 * n + 128, :] * ((dif + 128.0 * (j - i)) * scale)
        c_ref[128 * i:128 * i + 128, 128 * j:128 * j + 128] = -k
        c_ref[128 * j:128 * j + 128, 128 * i:128 * i + 128] = k.T
    for m in range(4):
        k = g_ref[128 * (28 + m):128 * (29 + m), :] * (dif * scale)
        up = jnp.where(bj > bi, k, 0.0)
        low = jnp.where(bj < bi, k, 0.0)
        a = 256 * m
        c_ref[a:a + 128, a:a + 128] = eye - (up - up.T)
        c_ref[a + 128:a + 256, a + 128:a + 256] = eye - (low - low.T)
    load_pair(t_ref, parts, c_ref, 1024)
    for ref in (w_ref, y_ref):
        ref[...] = jnp.zeros(ref.shape, BF)
    d_ref[...] = c_ref[0:128, 0:128]

    def columns(k):
        return pl.ds(pl.multiple_of(k * 128, 128), 128)

    def scaled(r, kc):
        y = dot(jnp.concatenate(split(c_ref[r, kc]), axis=1), w_ref[...])
        y = y[:, :128] + y[:, 128:]
        return y, jnp.concatenate(split(y) * 2, axis=1)

    def pivot_rows(kc, cs):
        hi, lo = split(c_ref[kc, cs])
        for i, x in enumerate((hi, hi, lo, lo)):
            a_ref[128 * i:128 * i + 128, cs] = x

    def update(r, cs):
        c_ref[r, cs] = c_ref[r, cs] - dot(y_ref[r, :], a_ref[:, cs])

    def step(first, k, _):
        before = columns(jnp.maximum(k - 1, 0))

        def work(p):
            each = 4 * (5 - first)
            if p * each % 16 >= each:
                return
            p = p * each // 16
            r = slice(256 * (p // 4 + first), 256 * (p // 4 + first) + 256)
            cs = slice(256 * (p % 4), 256 * (p % 4) + 256)
            if p < 4:
                pivot_rows(before, cs)
            if p % 4 == 0:
                y, y_ref[r, :] = scaled(r, before)
                c_ref[r, before] = jnp.where(k == 0, c_ref[r, before], y)
            update(r, cs)

        m = invert128([d_ref[8 * r:8 * r + 8, :] for r in range(16)], work)
        for r in range(16):
            d_ref[8 * r:8 * r + 8, :] = m[r]
        kc = columns(k)
        c_ref[kc, kc] = jnp.zeros((128, 128), F32)
        dh, dl = split(d_ref[...])
        w_ref[0:128, 0:128] = dh
        w_ref[128:256, 0:128] = dh
        w_ref[0:128, 128:256] = dl
        w_ref[128:256, 128:256] = dl
        nc = columns(jnp.minimum(k + 1, 7))
        hi, lo = split(c_ref[kc, nc])
        _, y = scaled(nc, kc)
        d_ref[...] = c_ref[nc, nc] - dot(y, jnp.concatenate([hi, hi, lo, lo], axis=0))

        def first_rows(i, _):
            r = slice(0, 256)
            y, y_ref[r, :] = scaled(r, kc)
            c_ref[r, kc] = y
            for c in range(0, 1024, 256):
                pivot_rows(kc, slice(c, c + 256))
                update(r, slice(c, c + 256))
            return 0

        lax.fori_loop(k, 1, first_rows, 0)
        return 0

    for first, start, stop in ((1, 0, 4), (2, 4, 6), (3, 6, 8)):
        lax.fori_loop(start, stop, functools.partial(step, first), 0)
    last = slice(896, 1024)
    y, y_ref[1024:1280, :] = scaled(slice(1024, 1280), last)
    c_ref[1024:1280, last] = y
    for c in range(0, 1024, 256):
        pivot_rows(last, slice(c, c + 256))
        update(slice(1024, 1280), slice(c, c + 256))
    load_pair(t_ref, parts, x_ref, 0)
    if n_parts == 1:
        for o_ref, half in zip(o_refs, (t_ref[5], 1 - t_ref[5])):
            cs = pl.ds(pl.multiple_of(half * 512, 512), 512)
            o_ref[...] = 2.0 * c_ref[1024:1280, cs] - x_ref[:, cs]
    else:
        for n in range(2):
            cs = slice(512 * n, 512 * n + 512)
            o_refs[0][n] = 2.0 * c_ref[1024:1280, cs] - x_ref[:, cs]


def solve(t, g, parts):
    half = jax.ShapeDtypeStruct((256, 512), F32)
    return vmem_call(
        functools.partial(solve_kern, len(parts)),
        (half, half) if len(parts) == 1 else jax.ShapeDtypeStruct((2, 256, 512), F32),
        1,
        [pltpu.VMEM((1280, 1024), F32), pltpu.VMEM((256, 1024), F32), pltpu.VMEM((128, 128), F32),
         pltpu.VMEM((256, 256), BF)] + [pltpu.VMEM((512, 1024), BF), pltpu.VMEM((1280, 512), BF)],
        "solve", t, g, *parts)


def comm_kern(g_ref, o_ref, r1, h, qa, qb, *rest):
    r2a, r3a, r2b, r3b = rest[:NA], rest[NA:2 * NA], rest[2 * NA], rest[2 * NA + 1]
    sems = rest[2 * NA + 2:]
    row = lax.axis_index("row")
    c = lax.rem(row, 2)
    y = lax.rem(row // 2, NY)
    z = row // (2 * NY)
    ys = [lax.rem(y + d, NY) for d in range(NY)]
    zs = [lax.rem(z + d, NZ) for d in range(NZ)]
    ydev = [{"row": (z * NY + ys[d]) * 2 + c} for d in range(NY)]
    zdev = [{"row": (zs[d] * NY + y) * 2 + c} for d in range(NZ)]
    other = {"row": (z * NY + y) * 2 + 1 - c}
    half = c * HALF

    def at(start, size):
        return pl.ds(pl.multiple_of(start, 8), size)

    barrier = pltpu.get_barrier_semaphore()
    for target in [other] + ydev[1:] + zdev[1:]:
        pl.semaphore_signal(barrier, inc=1, device_id=target, device_id_type=MESH)
    pl.semaphore_wait(barrier, NY + NZ - 1)

    sent = []

    def send(src, dst, pair, n, target):
        copy = pltpu.make_async_remote_copy(
            src_ref=src, dst_ref=dst, send_sem=sems[2 * pair].at[n], recv_sem=sems[2 * pair + 1].at[n],
            device_id=target, device_id_type=MESH)
        copy.start()
        sent.append(copy)
        return copy

    def came(copies):
        for copy in copies:
            copy.wait_recv()

    ya = [[at(PA * i + ys[d] * YA, YA) for d in range(NY)] for i in range(NA)]
    chunks = [ya[0][d] for d in YORDER] + [at(NA * PA, PB), ya[0][0]]
    chunks += [ya[i][d] for i in range(1, NA) for d in YORDER + (0,)]
    core = [send(g_ref.at[at((1 - c) * HALF + s.start, s.size)], r1.at[s], 0, n, other) for n, s in enumerate(chunks)]

    def add(s):
        h[s, :] = g_ref[at(half + s.start, s.size), :] + r1[s, :]

    def sum_y(i):
        out = []
        for d in YORDER:
            add(ya[i][d])
            out.append(send(h.at[ya[i][d]], r2a[i].at[d - 1], 6 + i, d - 1, ydev[d]))
        return out

    def sum_z(i):
        out = []
        for d in ZORDER + (0,):
            s = at(zs[d] * ZA, ZA)
            t = at(YA * i + zs[d] * ZA, ZA)
            qa[t, :] = ((h[at(PA * i + y * YA + zs[d] * ZA, ZA), :] + r2a[i][0, s, :])
                        + (r2a[i][1, s, :] + r2a[i][2, s, :]))
            if d:
                out.append(send(qa.at[t], r3a[i].at[d - 1], 6 + NA + i, d - 1, zdev[d]))
        return out

    came(core[:3])
    sums_ya = [sum_y(0)]
    came(core[3:4])
    sums_zb = []
    for d in ZORDER:
        s = at(NA * PA + zs[d] * ZB, ZB)
        add(s)
        sums_zb.append(send(h.at[s], r2b.at[d - 1], 1, d - 1, zdev[d]))
    add(at(NA * PA + z * ZB, ZB))
    came(core[4:5])
    add(ya[0][0])
    came(core[5:])
    for i in range(1, NA):
        add(ya[i][0])
    sums_ya += [sum_y(i) for i in range(1, NA)]

    came(sums_ya[0])
    sums_za = [sum_z(0)]
    came(sums_zb)
    total = h[at(NA * PA + z * ZB, ZB), :]
    for d in range(NZ - 1):
        total = total + r2b[d]
    qb[...] = total
    sums_yb = [send(qb.at[at(ys[d] * YB, YB)], r3b.at[d - 1], 2, d - 1, ydev[d]) for d in YORDER]
    for i in range(1, NA):
        came(sums_ya[i])
        sums_za.append(sum_z(i))

    came(sums_yb)
    mine = at(half + NA * PA + z * ZB + y * YB, YB)
    o_ref[mine, :] = (qb[at(y * YB, YB), :] + r3b[0]) + (r3b[1] + r3b[2])
    back_yb = [send(o_ref.at[mine], o_ref.at[mine], 3, d - 1, ydev[d]) for d in YORDER]

    back_za = []
    for i in range(NA):
        came(sums_za[i])
        total = qa[at(YA * i + z * ZA, ZA), :]
        for d in range(NZ - 1):
            total = total + r3a[i][d]
        mine = at(half + PA * i + y * YA + z * ZA, ZA)
        o_ref[mine, :] = total
        back_za.append([send(o_ref.at[mine], o_ref.at[mine], 6 + 2 * NA + i, d - 1, zdev[d]) for d in ZORDER])

    back_ya, back = [], []
    for i in range(NA):
        came(back_za[i])
        own = at(half + PA * i + y * YA, YA)
        back_ya.append([send(o_ref.at[own], o_ref.at[own], 6 + 3 * NA + i, d - 1, ydev[d]) for d in YORDER])
        back.append(send(o_ref.at[own], o_ref.at[own], 5, 4 * i, other))
    came(back_yb)
    own = at(half + NA * PA + z * ZB, ZB)
    back_zb = [send(o_ref.at[own], o_ref.at[own], 4, d - 1, zdev[d]) for d in ZORDER]
    for i in range(NA):
        for n, d in enumerate(YORDER):
            back_ya[i][n].wait_recv()
            part = at(half + PA * i + lax.rem(y + NY - d, NY) * YA, YA)
            back.append(send(o_ref.at[part], o_ref.at[part], 5, 4 * i + 1 + n, other))
    came(back_zb)
    part = at(half + NA * PA, PB)
    back.append(send(o_ref.at[part], o_ref.at[part], 5, 4 * NA, other))
    came(back)
    for copy in sent:
        copy.wait_send()


def comm(g):
    counts = (4 * NA + 1, 7, 3, 3, 7, 4 * NA + 1) + (3,) * NA + (7,) * (2 * NA) + (3,) * NA
    buffers = ((HALF,), (HALF,), (NA * YA,), (ZB,)) + ((3, YA),) * NA + ((7, ZA),) * NA + ((7, ZB), (3, YB))
    return pl.pallas_call(
        comm_kern,
        out_shape=jax.ShapeDtypeStruct((2 * HALF, 128), F32),
        in_specs=[pl.BlockSpec(memory_space=pltpu.VMEM)],
        out_specs=pl.BlockSpec(memory_space=pltpu.VMEM),
        scratch_shapes=[pltpu.VMEM(b + (128,), F32) for b in buffers]
        + [pltpu.SemaphoreType.DMA((n,)) for n in counts for _ in range(2)],
        compiler_params=pltpu.CompilerParams(
            vmem_limit_bytes=24 * 2**20, collective_id=0, has_side_effects=True),
        name="comm")(g)


def swap_kern(n_blocks, t_ref, x_ref, o_ref, *rest):
    mids, outs, (ss1, rs1, ss2, rs2) = rest[:NS], rest[NS:2 * NS], rest[2 * NS:]
    me = lax.axis_index("pair")
    others = [lax.rem(me + d, 4) for d in range(4)]
    barrier = pltpu.get_barrier_semaphore()
    for d in (2, 1, 3):
        pl.semaphore_signal(barrier, inc=1, device_id={"pair": others[d]}, device_id_type=MESH)
    pl.semaphore_wait(barrier, 3)
    size = 64 // NS

    def rows(j, i):
        return pl.ds(pl.multiple_of(64 * j + size * i, size), size)

    def send(src, dst, ss, rs, i, d):
        copy = pltpu.make_async_remote_copy(
            src_ref=src, dst_ref=dst, send_sem=ss.at[i, d - 1], recv_sem=rs.at[i, d - 1],
            device_id={"pair": others[d]}, device_id_type=MESH)
        copy.start()
        return copy

    there = [[send(x_ref.at[:, rows(others[d], i), :], mids[i].at[:, me], ss1, rs1, i, d) for d in (2, 1, 3)]
             for i in range(NS)]
    for i in range(NS):
        mids[i][:, me] = x_ref[:, rows(me, i), :]
    back = []
    for i in range(NS):
        for copy in there[i]:
            copy.wait_recv()
        for d in (2, 1, 3, 0):
            for n in range(n_blocks):
                at = t_ref[8 + n_blocks * others[d] + n] if n_blocks == 2 else t_ref[others[d]]
                block = mids[i][at // 4, at % 4]
                if d:
                    outs[i][d - 1, :, 512 * n:512 * n + 512] = block
                else:
                    o_ref[rows(me, i), 512 * n:512 * n + 512] = block
            if d:
                back.append(send(outs[i].at[d - 1], o_ref.at[rows(me, i), :], ss2, rs2, i, d))
    for copy in back:
        copy.wait_recv()
    for copies in there + [back]:
        for copy in copies:
            copy.wait_send()


def swap(t, x):
    n = x.shape[0]
    vm = pl.BlockSpec(memory_space=pltpu.VMEM)
    return pl.pallas_call(
        functools.partial(swap_kern, n),
        out_shape=jax.ShapeDtypeStruct((256, 512 * n), F32),
        in_specs=[pl.BlockSpec(memory_space=pltpu.SMEM), vm],
        out_specs=vm,
        scratch_shapes=[pltpu.VMEM((n, 4, 64 // NS, 512), F32)] * NS + [pltpu.VMEM((3, 64 // NS, 512 * n), F32)] * NS
        + [pltpu.SemaphoreType.DMA((NS, 3))] * 4,
        compiler_params=pltpu.CompilerParams(
            vmem_limit_bytes=16 * 2**20, collective_id=n, has_side_effects=True),
        name="swap")(t, x)


def route(plan_ref, t_ref):
    me = lax.axis_index("pair")

    def pick(values, n):
        out = values[0]
        for i in range(1, len(values)):
            out = jnp.where(n == i, values[i], out)
        return out

    def place(values, v):
        return sum(i * (x == v).astype(jnp.int32) for i, x in enumerate(values))

    first = [plan_ref[0, 2 * q] for q in range(4)]
    second = [plan_ref[0, 2 * q + 1] for q in range(4)]
    one = [jnp.left_shift(1, v >> 1) for v in first]
    two = [jnp.left_shift(1, v >> 1) for v in second]
    best = jnp.int32(0)
    for mask in range(16):
        seen = 0
        for q in range(4):
            seen = seen | (two[q] if mask >> q & 1 else one[q])
        best = jnp.where(seen == 15, mask, best)
    bit = [jnp.right_shift(best, q) & 1 for q in range(4)]
    kept = [jnp.where(bit[q] == 1, second[q], first[q]) for q in range(4)]
    moved = [jnp.where(bit[q] == 1, first[q], second[q]) for q in range(4)]
    home = [v >> 1 for v in kept]
    for d in range(4):
        t_ref[d] = pick(moved, place(home, d)) >> 1
    mine = place(home, me)
    t_ref[4] = pick(bit, mine)
    t_ref[5] = pick(kept, mine) & 1
    t_ref[6] = 0
    t_ref[7] = 0
    where = [4 * (i % 2) + home[i // 2] for i in range(8)]
    blocks = [plan_ref[0, i] for i in range(8)]
    for p in range(8):
        t_ref[8 + p] = pick(where, place(blocks, plan_ref[1, p]))


def body(matrix, plan):
    g, t = gram(plan, (matrix,))
    keep, away = solve(t, comm(g), (matrix,))
    parts = (keep, swap(t, away[None]))
    return swap(t, solve(t, comm(gram(t, parts)), parts))


def solution(mesh):
    placed = (P("row", "pair"), P())
    return jax.shard_map(
        body, mesh=mesh, in_specs=placed, out_specs=P("row", "pair"), check_vma=False
    )
```

```python
import functools
import itertools

import jax
import jax.numpy as jnp
from jax import lax
from jax.experimental import pallas as pl
from jax.experimental.pallas import tpu as pltpu
from jax.sharding import PartitionSpec as P

F32 = jnp.float32
BF = jnp.bfloat16
MESH = pl.DeviceIdType.MESH
OFF = [(i, j) for i in range(8) for j in range(i + 1, 8)]
NZ, NY = 8, 4
NA, HALF, PA, PB = 2, 2048, 768, 512
YA, ZA, ZB, YB = PA // NY, PA // NY // NZ, PB // NZ, PB // NZ // NY
YORDER = (2, 1, 3)
ZORDER = (4, 3, 5, 2, 6, 1, 7)
NS = 2


def split(x):
    hi = x.astype(BF)
    return hi, (x - hi.astype(F32)).astype(BF)


def dot(a, b):
    return jnp.dot(a, b, preferred_element_type=F32)


def iotas(n, m):
    shape = (n, m)
    return lax.broadcasted_iota(jnp.int32, shape, 0), lax.broadcasted_iota(jnp.int32, shape, 1)


def vmem_call(kern, outs, n_smem, scratch, name, *args):
    vm = pl.BlockSpec(memory_space=pltpu.VMEM)
    sm = pl.BlockSpec(memory_space=pltpu.SMEM)
    return pl.pallas_call(
        kern,
        out_shape=outs,
        in_specs=[sm] * n_smem + [vm] * (len(args) - n_smem),
        out_specs=jax.tree.map(lambda out: sm if out.dtype == jnp.int32 else vm, outs),
        scratch_shapes=scratch,
        compiler_params=pltpu.CompilerParams(vmem_limit_bytes=32 * 2**20),
        name=name,
    )(*args)


def load_pair(t_ref, parts, dst, row0):
    if len(parts) == 1:
        dst[row0:row0 + 256, :] = parts[0][...]
        return
    at = t_ref[4] * 512
    dst[row0:row0 + 256, pl.ds(pl.multiple_of(at, 512), 512)] = parts[0][...]
    dst[row0:row0 + 256, pl.ds(pl.multiple_of(512 - at, 512), 512)] = parts[1][...]


def gram_kern(n_parts, t_ref, *refs):
    parts = refs[:n_parts]
    if n_parts == 1:
        g_ref, table_ref, x_ref, ph, plo, th, tl = refs[n_parts:]
        route(t_ref, table_ref)
    else:
        g_ref, x_ref, ph, plo, th, tl = refs[n_parts:]
    load_pair(t_ref, parts, x_ref, 0)
    for c in range(0, 1024, 256):
        x = x_ref[:, c:c + 256]
        ph[:, c:c + 256], plo[:, c:c + 256] = split(x)
        th[c:c + 256, :], tl[c:c + 256, :] = split(x.T)
    bi, bj = iotas(128, 128)
    for i in range(4):
        r = slice(256 * i, 256 * i + 256)
        for j in range(i, 4):
            c = slice(256 * j, 256 * j + 256)
            g = dot(th[r, :], ph[:, c]) + (dot(th[r, :], plo[:, c]) + dot(tl[r, :], ph[:, c]))
            for u in range(2):
                for v in range(2):
                    if (2 * i + u, 2 * j + v) in OFF:
                        n = 128 * OFF.index((2 * i + u, 2 * j + v))
                        g_ref[n:n + 128, :] = g[128 * u:128 * u + 128, 128 * v:128 * v + 128]
            if i == j:
                n = 128 * (28 + i)
                g_ref[n:n + 128, :] = jnp.where(bj > bi, g[:128, :128], g[128:, 128:])


def gram(t, parts):
    out = jax.ShapeDtypeStruct((4096, 128), F32)
    return vmem_call(
        functools.partial(gram_kern, len(parts)),
        (out, jax.ShapeDtypeStruct((16,), jnp.int32)) if len(parts) == 1 else out,
        1,
        [pltpu.VMEM((256, 1024), F32)] + [pltpu.VMEM((256, 1024), BF)] * 2 + [pltpu.VMEM((1024, 256), BF)] * 2,
        "gram", t, *parts)


def lane_bcast(x, c):
    return jnp.broadcast_to(x[:, c:c + 1], (8, 128))


def row_bcast(x, s):
    return jnp.broadcast_to(x[s:s + 1, :], (8, 128))


def total8(t):
    return ((t[0] + t[1]) + (t[2] + t[3])) + ((t[4] + t[5]) + (t[6] + t[7]))


def panel_product(m, n, p):
    x0, x1 = split(jnp.concatenate(m, axis=0))
    zero = [jnp.zeros((8, 128), F32)]
    y0, y1 = split(jnp.concatenate(zero * p + [n] + zero * (15 - p), axis=0))
    top = jnp.concatenate([y0, y1], axis=1)
    u = dot(jnp.concatenate([x0, x1], axis=1), jnp.concatenate([top, top], axis=0))
    return u[:, :128] + u[:, 128:]


def invert128(m, work):
    sub, lane = iotas(8, 128)
    m = list(m)
    e = [lane_bcast(m[0], k) for k in range(8)]
    for p in range(16):
        nxt = (p + 1) % 16
        left = [lane_bcast(m[nxt], 8 * p + k) for k in range(8)]
        work(p)
        upper = [lane_bcast(m[p], 8 * p + 8 + k) for k in range(8 if p < 15 else 0)]
        corner = [lane_bcast(m[nxt], 8 * p + 8 + k) for k in range(8 if p < 15 else 0)]
        after = (p + 2) % 16
        left2 = [lane_bcast(m[after], 8 * p + k) for k in range(8)]
        inside = (lane >= 8 * p) & (lane < 8 * p + 8)
        for s in range(0, 8, 2):
            u, v = e[s], e[s + 1]
            a, b, c, d = row_bcast(u, s), row_bcast(v, s), row_bcast(u, s + 1), row_bcast(v, s + 1)
            rd = 1.0 / (a * d - b * c)
            a, b, c, d = a * rd, b * rd, c * rd, d * rd
            r0, r1 = sub == s, sub == s + 1
            both = (sub >= s) & (sub <= s + 1)
            u, v = jnp.where(both, jnp.where(r0, -1.0, 0.0), u), jnp.where(both, jnp.where(r1, -1.0, 0.0), v)
            new = list(e)
            for j in range(8):
                if j == s:
                    new[j] = v * c - u * d
                elif j == s + 1:
                    new[j] = u * b - v * a
                else:
                    x0, x1 = row_bcast(e[j], s), row_bcast(e[j], s + 1)
                    new[j] = jnp.where(both, 0.0, e[j]) - u * (d * x0 - b * x1) - v * (a * x1 - c * x0)
            e = new
        ahead = []
        for k in range(len(corner)):
            x = total8([e[i] * row_bcast(upper[k], i) for i in range(8)])
            ahead.append(corner[k] - total8([left[i] * row_bcast(x, i) for i in range(8)]))
        mp = jnp.where(inside, jnp.where(lane - 8 * p == sub, 1.0, 0.0), m[p])
        n = total8([e[k] * row_bcast(mp, k) for k in range(8)])
        soon = jnp.where(inside, 0.0, m[nxt]) - total8([left[k] * row_bcast(n, k) for k in range(8)])
        soon2 = jnp.where(inside, 0.0, m[after]) - total8([left2[k] * row_bcast(n, k) for k in range(8)])
        e = ahead
        t = panel_product(m, n, p)
        for r in range(16):
            m[r] = n if r == p else soon if r == nxt else soon2 if r == after else jnp.where(inside, 0.0, m[r]) - t[8 * r:8 * r + 8, :]
    return m


def solve_kern(n_parts, t_ref, g_ref, *refs):
    parts = refs[:n_parts]
    o_refs, (c_ref, x_ref, d_ref, w_ref, a_ref, y_ref) = refs[n_parts:-6], refs[-6:]
    bi, bj = iotas(128, 128)
    dif = (bj - bi).astype(F32)
    eye = jnp.where(bi == bj, 1.0, 0.0)
    scale = 1.0 / (1024 * 128 * 2)
    for n, (i, j) in enumerate(OFF):
        k = g_ref[128 * n:128 * n + 128, :] * ((dif + 128.0 * (j - i)) * scale)
        c_ref[128 * i:128 * i + 128, 128 * j:128 * j + 128] = -k
        c_ref[128 * j:128 * j + 128, 128 * i:128 * i + 128] = k.T
    for m in range(4):
        k = g_ref[128 * (28 + m):128 * (29 + m), :] * (dif * scale)
        up = jnp.where(bj > bi, k, 0.0)
        low = jnp.where(bj < bi, k, 0.0)
        a = 256 * m
        c_ref[a:a + 128, a:a + 128] = eye - (up - up.T)
        c_ref[a + 128:a + 256, a + 128:a + 256] = eye - (low - low.T)
    load_pair(t_ref, parts, c_ref, 1024)
    for ref in (w_ref, y_ref):
        ref[...] = jnp.zeros(ref.shape, BF)
    d_ref[...] = c_ref[0:128, 0:128]

    def columns(k):
        return pl.ds(pl.multiple_of(k * 128, 128), 128)

    def scaled(r, kc):
        y = dot(jnp.concatenate(split(c_ref[r, kc]), axis=1), w_ref[...])
        y = y[:, :128] + y[:, 128:]
        return y, jnp.concatenate(split(y) * 2, axis=1)

    def pivot_rows(kc, cs):
        hi, lo = split(c_ref[kc, cs])
        for i, x in enumerate((hi, hi, lo, lo)):
            a_ref[128 * i:128 * i + 128, cs] = x

    def update(r, cs):
        c_ref[r, cs] = c_ref[r, cs] - dot(y_ref[r, :], a_ref[:, cs])

    def step(first, k, _):
        before = columns(jnp.maximum(k - 1, 0))

        def work(p):
            each = 4 * (5 - first)
            if p * each % 16 >= each:
                return
            p = p * each // 16
            r = slice(256 * (p // 4 + first), 256 * (p // 4 + first) + 256)
            cs = slice(256 * (p % 4), 256 * (p % 4) + 256)
            if p < 4:
                pivot_rows(before, cs)
            if p % 4 == 0:
                y, y_ref[r, :] = scaled(r, before)
                c_ref[r, before] = jnp.where(k == 0, c_ref[r, before], y)
            update(r, cs)

        m = invert128([d_ref[8 * r:8 * r + 8, :] for r in range(16)], work)
        for r in range(16):
            d_ref[8 * r:8 * r + 8, :] = m[r]
        kc = columns(k)
        c_ref[kc, kc] = jnp.zeros((128, 128), F32)
        dh, dl = split(d_ref[...])
        w_ref[0:128, 0:128] = dh
        w_ref[128:256, 0:128] = dh
        w_ref[0:128, 128:256] = dl
        w_ref[128:256, 128:256] = dl
        nc = columns(jnp.minimum(k + 1, 7))
        hi, lo = split(c_ref[kc, nc])
        _, y = scaled(nc, kc)
        d_ref[...] = c_ref[nc, nc] - dot(y, jnp.concatenate([hi, hi, lo, lo], axis=0))

        def first_rows(i, _):
            r = slice(0, 256)
            y, y_ref[r, :] = scaled(r, kc)
            c_ref[r, kc] = y
            for c in range(0, 1024, 256):
                pivot_rows(kc, slice(c, c + 256))
                update(r, slice(c, c + 256))
            return 0

        lax.fori_loop(k, 1, first_rows, 0)
        return 0

    for first, start, stop in ((1, 0, 4), (2, 4, 6), (3, 6, 8)):
        lax.fori_loop(start, stop, functools.partial(step, first), 0)
    last = slice(896, 1024)
    y, y_ref[1024:1280, :] = scaled(slice(1024, 1280), last)
    c_ref[1024:1280, last] = y
    for c in range(0, 1024, 256):
        pivot_rows(last, slice(c, c + 256))
        update(slice(1024, 1280), slice(c, c + 256))
    load_pair(t_ref, parts, x_ref, 0)
    if n_parts == 1:
        for o_ref, half in zip(o_refs, (t_ref[5], 1 - t_ref[5])):
            cs = pl.ds(pl.multiple_of(half * 512, 512), 512)
            o_ref[...] = 2.0 * c_ref[1024:1280, cs] - x_ref[:, cs]
    else:
        for n in range(2):
            cs = slice(512 * n, 512 * n + 512)
            o_refs[0][n] = 2.0 * c_ref[1024:1280, cs] - x_ref[:, cs]


def solve(t, g, parts):
    half = jax.ShapeDtypeStruct((256, 512), F32)
    return vmem_call(
        functools.partial(solve_kern, len(parts)),
        (half, half) if len(parts) == 1 else jax.ShapeDtypeStruct((2, 256, 512), F32),
        1,
        [pltpu.VMEM((1280, 1024), F32), pltpu.VMEM((256, 1024), F32), pltpu.VMEM((128, 128), F32),
         pltpu.VMEM((256, 256), BF)] + [pltpu.VMEM((512, 1024), BF), pltpu.VMEM((1280, 512), BF)],
        "solve", t, g, *parts)


def comm_kern(g_ref, o_ref, r1, h, qa, qb, *rest):
    r2a, r3a, r2b, r3b = rest[:NA], rest[NA:2 * NA], rest[2 * NA], rest[2 * NA + 1]
    sems = rest[2 * NA + 2:]
    row = lax.axis_index("row")
    c = lax.rem(row, 2)
    y = lax.rem(row // 2, NY)
    z = row // (2 * NY)
    ys = [lax.rem(y + d, NY) for d in range(NY)]
    zs = [lax.rem(z + d, NZ) for d in range(NZ)]
    ydev = [{"row": (z * NY + ys[d]) * 2 + c} for d in range(NY)]
    zdev = [{"row": (zs[d] * NY + y) * 2 + c} for d in range(NZ)]
    other = {"row": (z * NY + y) * 2 + 1 - c}
    half = c * HALF

    def at(start, size):
        return pl.ds(pl.multiple_of(start, 8), size)

    barrier = pltpu.get_barrier_semaphore()
    for target in [other] + ydev[1:] + zdev[1:]:
        pl.semaphore_signal(barrier, inc=1, device_id=target, device_id_type=MESH)
    pl.semaphore_wait(barrier, NY + NZ - 1)

    sent = []

    def send(src, dst, pair, n, target):
        copy = pltpu.make_async_remote_copy(
            src_ref=src, dst_ref=dst, send_sem=sems[2 * pair].at[n], recv_sem=sems[2 * pair + 1].at[n],
            device_id=target, device_id_type=MESH)
        copy.start()
        sent.append(copy)
        return copy

    def came(copies):
        for copy in copies:
            copy.wait_recv()

    ya = [[at(PA * i + ys[d] * YA, YA) for d in range(NY)] for i in range(NA)]
    chunks = [ya[0][d] for d in YORDER] + [at(NA * PA, PB), ya[0][0]]
    chunks += [ya[i][d] for i in range(1, NA) for d in YORDER + (0,)]
    core = [send(g_ref.at[at((1 - c) * HALF + s.start, s.size)], r1.at[s], 0, n, other) for n, s in enumerate(chunks)]

    def add(s):
        h[s, :] = g_ref[at(half + s.start, s.size), :] + r1[s, :]

    def sum_y(i):
        out = []
        for n, d in enumerate(YORDER):
            if i == 0:
                came(core[n:n + 1])
            add(ya[i][d])
            out.append(send(h.at[ya[i][d]], r2a[i].at[d - 1], 6 + i, d - 1, ydev[d]))
        return out

    def sum_z(i):
        out = []
        for d in ZORDER + (0,):
            s = at(zs[d] * ZA, ZA)
            t = at(YA * i + zs[d] * ZA, ZA)
            qa[t, :] = ((h[at(PA * i + y * YA + zs[d] * ZA, ZA), :] + r2a[i][0, s, :])
                        + (r2a[i][1, s, :] + r2a[i][2, s, :]))
            if d:
                out.append(send(qa.at[t], r3a[i].at[d - 1], 6 + NA + i, d - 1, zdev[d]))
        return out

    sums_ya = [sum_y(0)]
    came(core[3:4])
    sums_zb = []
    for d in ZORDER:
        s = at(NA * PA + zs[d] * ZB, ZB)
        add(s)
        sums_zb.append(send(h.at[s], r2b.at[d - 1], 1, d - 1, zdev[d]))
    add(at(NA * PA + z * ZB, ZB))
    came(core[4:5])
    add(ya[0][0])
    came(core[5:])
    for i in range(1, NA):
        add(ya[i][0])
    sums_ya += [sum_y(i) for i in range(1, NA)]

    came(sums_ya[0])
    sums_za = [sum_z(0)]
    came(sums_zb)
    total = h[at(NA * PA + z * ZB, ZB), :]
    for d in range(NZ - 1):
        total = total + r2b[d]
    qb[...] = total
    sums_yb = [send(qb.at[at(ys[d] * YB, YB)], r3b.at[d - 1], 2, d - 1, ydev[d]) for d in YORDER]
    for i in range(1, NA):
        came(sums_ya[i])
        sums_za.append(sum_z(i))

    came(sums_yb)
    mine = at(half + NA * PA + z * ZB + y * YB, YB)
    o_ref[mine, :] = (qb[at(y * YB, YB), :] + r3b[0]) + (r3b[1] + r3b[2])
    back_yb = [send(o_ref.at[mine], o_ref.at[mine], 3, d - 1, ydev[d]) for d in YORDER]

    back_za = []
    for i in range(NA):
        came(sums_za[i])
        total = qa[at(YA * i + z * ZA, ZA), :]
        for d in range(NZ - 1):
            total = total + r3a[i][d]
        mine = at(half + PA * i + y * YA + z * ZA, ZA)
        o_ref[mine, :] = total
        back_za.append([send(o_ref.at[mine], o_ref.at[mine], 6 + 2 * NA + i, d - 1, zdev[d]) for d in ZORDER])

    back_ya, back = [], []
    for i in range(NA):
        came(back_za[i])
        own = at(half + PA * i + y * YA, YA)
        back_ya.append([send(o_ref.at[own], o_ref.at[own], 6 + 3 * NA + i, d - 1, ydev[d]) for d in YORDER])
        back.append(send(o_ref.at[own], o_ref.at[own], 5, 4 * i, other))
    came(back_yb)
    own = at(half + NA * PA + z * ZB, ZB)
    back_zb = [send(o_ref.at[own], o_ref.at[own], 4, d - 1, zdev[d]) for d in ZORDER]
    for i in range(NA):
        for n, d in enumerate(YORDER):
            back_ya[i][n].wait_recv()
            part = at(half + PA * i + lax.rem(y + NY - d, NY) * YA, YA)
            back.append(send(o_ref.at[part], o_ref.at[part], 5, 4 * i + 1 + n, other))
    came(back_zb)
    part = at(half + NA * PA, PB)
    back.append(send(o_ref.at[part], o_ref.at[part], 5, 4 * NA, other))
    came(back)
    for copy in sent:
        copy.wait_send()


def comm(g):
    counts = (4 * NA + 1, 7, 3, 3, 7, 4 * NA + 1) + (3,) * NA + (7,) * (2 * NA) + (3,) * NA
    buffers = ((HALF,), (HALF,), (NA * YA,), (ZB,)) + ((3, YA),) * NA + ((7, ZA),) * NA + ((7, ZB), (3, YB))
    return pl.pallas_call(
        comm_kern,
        out_shape=jax.ShapeDtypeStruct((2 * HALF, 128), F32),
        in_specs=[pl.BlockSpec(memory_space=pltpu.VMEM)],
        out_specs=pl.BlockSpec(memory_space=pltpu.VMEM),
        scratch_shapes=[pltpu.VMEM(b + (128,), F32) for b in buffers]
        + [pltpu.SemaphoreType.DMA((n,)) for n in counts for _ in range(2)],
        compiler_params=pltpu.CompilerParams(
            vmem_limit_bytes=24 * 2**20, collective_id=0, has_side_effects=True),
        name="comm")(g)


def swap_kern(n_blocks, t_ref, x_ref, o_ref, *rest):
    mids, outs, (ss1, rs1, ss2, rs2) = rest[:NS], rest[NS:2 * NS], rest[2 * NS:]
    me = lax.axis_index("pair")
    others = [lax.rem(me + d, 4) for d in range(4)]
    barrier = pltpu.get_barrier_semaphore()
    for d in (2, 1, 3):
        pl.semaphore_signal(barrier, inc=1, device_id={"pair": others[d]}, device_id_type=MESH)
    pl.semaphore_wait(barrier, 3)
    size = 64 // NS

    def rows(j, i):
        return pl.ds(pl.multiple_of(64 * j + size * i, size), size)

    def send(src, dst, ss, rs, i, d):
        copy = pltpu.make_async_remote_copy(
            src_ref=src, dst_ref=dst, send_sem=ss.at[i, d - 1], recv_sem=rs.at[i, d - 1],
            device_id={"pair": others[d]}, device_id_type=MESH)
        copy.start()
        return copy

    there = [[send(x_ref.at[:, rows(others[d], i), :], mids[i].at[:, me], ss1, rs1, i, d) for d in (2, 1, 3)]
             for i in range(NS)]
    for i in range(NS):
        mids[i][:, me] = x_ref[:, rows(me, i), :]
    back = []
    for i in range(NS):
        for copy in there[i]:
            copy.wait_recv()
        for d in (2, 1, 3, 0):
            for n in range(n_blocks):
                at = t_ref[8 + n_blocks * others[d] + n] if n_blocks == 2 else t_ref[others[d]]
                block = mids[i][at // 4, at % 4]
                if d:
                    outs[i][d - 1, :, 512 * n:512 * n + 512] = block
                else:
                    o_ref[rows(me, i), 512 * n:512 * n + 512] = block
            if d:
                back.append(send(outs[i].at[d - 1], o_ref.at[rows(me, i), :], ss2, rs2, i, d))
    for copy in back:
        copy.wait_recv()
    for copies in there + [back]:
        for copy in copies:
            copy.wait_send()


def swap(t, x):
    n = x.shape[0]
    vm = pl.BlockSpec(memory_space=pltpu.VMEM)
    return pl.pallas_call(
        functools.partial(swap_kern, n),
        out_shape=jax.ShapeDtypeStruct((256, 512 * n), F32),
        in_specs=[pl.BlockSpec(memory_space=pltpu.SMEM), vm],
        out_specs=vm,
        scratch_shapes=[pltpu.VMEM((n, 4, 64 // NS, 512), F32)] * NS + [pltpu.VMEM((3, 64 // NS, 512 * n), F32)] * NS
        + [pltpu.SemaphoreType.DMA((NS, 3))] * 4,
        compiler_params=pltpu.CompilerParams(
            vmem_limit_bytes=16 * 2**20, collective_id=n, has_side_effects=True),
        name="swap")(t, x)


def route(plan_ref, t_ref):
    me = lax.axis_index("pair")

    def pick(values, n):
        out = values[0]
        for i in range(1, len(values)):
            out = jnp.where(n == i, values[i], out)
        return out

    def place(values, v):
        return sum(i * (x == v).astype(jnp.int32) for i, x in enumerate(values))

    first = [plan_ref[0, 2 * q] for q in range(4)]
    second = [plan_ref[0, 2 * q + 1] for q in range(4)]
    one = [jnp.left_shift(1, v >> 1) for v in first]
    two = [jnp.left_shift(1, v >> 1) for v in second]
    best = jnp.int32(0)
    for mask in range(16):
        seen = 0
        for q in range(4):
            seen = seen | (two[q] if mask >> q & 1 else one[q])
        best = jnp.where(seen == 15, mask, best)
    bit = [jnp.right_shift(best, q) & 1 for q in range(4)]
    kept = [jnp.where(bit[q] == 1, second[q], first[q]) for q in range(4)]
    moved = [jnp.where(bit[q] == 1, first[q], second[q]) for q in range(4)]
    home = [v >> 1 for v in kept]
    for d in range(4):
        t_ref[d] = pick(moved, place(home, d)) >> 1
    mine = place(home, me)
    t_ref[4] = pick(bit, mine)
    t_ref[5] = pick(kept, mine) & 1
    t_ref[6] = 0
    t_ref[7] = 0
    where = [4 * (i % 2) + home[i // 2] for i in range(8)]
    blocks = [plan_ref[0, i] for i in range(8)]
    for p in range(8):
        t_ref[8 + p] = pick(where, place(blocks, plan_ref[1, p]))


def body(matrix, plan):
    g, t = gram(plan, (matrix,))
    keep, away = solve(t, comm(g), (matrix,))
    parts = (keep, swap(t, away[None]))
    return swap(t, solve(t, comm(gram(t, parts)), parts))


def solution(mesh):
    placed = (P("row", "pair"), P())
    return jax.shard_map(
        body, mesh=mesh, in_specs=placed, out_specs=P("row", "pair"), check_vma=False
    )
```
